128 devices in a mesh: row: 16 (over y, x), col: 8 (over z, core).
Axes of the slice: x: 4, y: 4, z: 4, core: 2. Of those that a mesh axis runs over, the one named last changes fastest.
Arguments:
- right_side: float32 [512, 32, 256], P(('row', 'col')), may hold values from -70 to 70
- diag_term: float32 [512, 256], P(('row', 'col')), may hold values from 2.5 to 8
- near_pairs: int32 [3, 8192], P(None, ('row', 'col')), may hold values from 0 to 511, as said below
- near_tiles: bfloat16 [8192, 256, 256], P(('row', 'col')), may hold values from -0.0390625 to 0.0390625
- far_pairs: int32 [3, 12288], P(None, ('row', 'col')), may hold values from 0 to 511, as said below
- far_factors: bfloat16 [12288, 2, 32, 256], P(('row', 'col')), may hold values from -0.0625 to 0.0625
Outputs:
- solution_field: float32 [512, 32, 256], P(('row', 'col'))
- residual: float32 [512, 32, 256], P(('row', 'col'))
The draws below stay inside these ranges and needn't reach their ends.
Inputs may be any that keep to these rules, and one draw needn't show every extreme that they name: `near_pairs`: row 0 holds each slot's row cluster, row 1 its column cluster, row 2 a 1 for a live pair and 0 for an empty slot. The 64 slots of one device lie together in device order (row index slowest); its live slots come first, and some device has all 64 live. A slot's row cluster lies in the block of 32 clusters of its device's row index; its column cluster is no smaller, less than 4 clusters away, and before the end of the next block. `far_pairs`: row 0 holds each slot's row cluster, row 1 its column cluster, row 2 a 1 for a live pair and 0 for an empty slot. The 96 slots of one device lie together in device order (row index slowest); its live slots come first, and some device has all 96 live. A slot's row cluster lies in the block of 32 clusters of its device's row index; its column cluster is no smaller and lies before the end of the next block.
All inputs are finite; a program needn't handle non-finite values.
Results may differ from the reference program's by a relative error of at most 0.0033.
Values may be sent and summed in bfloat16 or wider, within the bound.
A program may use at most 64 MiB of HBM per device.

```python
import math
import jax
import jax.numpy as jnp
from jax import lax

CL = 256
RK = 32
NRHS = 32
NEAR_DEV = 64
FAR_DEV = 96
ITERS = 3
NEAR_REACH = 4
CPG = 32
NCLUST = 512
NNEAR = 8192
NFAR = 12288
N_COL = 8
DEVICES = 128


def pair_table(key, slot_count, reach_low, reach_high):
    slot_total = slot_count * DEVICES
    key_live, key_full, key_chosen, key_row, key_col = jax.random.split(key, 5)
    device_of = jnp.arange(slot_total, dtype=jnp.int32) // slot_count
    slot_of = jnp.arange(slot_total, dtype=jnp.int32) % slot_count
    live_count = jax.random.randint(key_live, (DEVICES,), slot_count // 8, slot_count // 2 + 1)
    full_device = jax.random.randint(key_full, (DEVICES,), 0, 8) == 0
    chosen_device = jax.random.randint(key_chosen, (), 0, DEVICES)
    full_device = full_device | (jnp.arange(DEVICES, dtype=jnp.int32) == chosen_device)
    live_count = jnp.where(full_device, slot_count, live_count)
    live_flag = (slot_of < live_count[device_of]).astype(jnp.int32)
    group_start = device_of // N_COL * CPG
    row_id = group_start + jax.random.randint(key_row, (slot_total,), 0, CPG)
    last_column = jnp.minimum(group_start + 2 * CPG, NCLUST) - 1
    col_id = jnp.minimum(row_id + jax.random.randint(key_col, (slot_total,), reach_low, reach_high), last_column)
    return jnp.stack([row_id, col_id, live_flag]).astype(jnp.int32)


def draw_near_pairs(key, part):
    key = jax.random.fold_in(key, 3)
    return pair_table(key, NEAR_DEV, 0, NEAR_REACH)


def draw_far_pairs(key, part):
    key = jax.random.fold_in(key, 5)
    return pair_table(key, FAR_DEV, 1, CPG + 1)


def draw_right_side(key, part):
    key = jax.random.fold_in(key, 7)
    key_noise, key_scale = jax.random.split(key, 2)
    position = jnp.arange(NCLUST, dtype=jnp.float32) / max(NCLUST - 1, 1)
    row_scale = jnp.exp(jax.random.uniform(key_scale, (NCLUST, NRHS, 1), minval=0.0, maxval=math.log(10.0)))
    rise = jnp.exp(math.log(3.0) * position)
    noise = jnp.clip(jax.random.normal(key_noise, (NCLUST, NRHS, CL)), -5.0, 5.0)
    return (0.2 * noise * row_scale * rise[:, None, None]).astype(jnp.float32)


def levels(own_key, dims, shards, low, largest):
    gain = 1.0
    for dim, blocks in shards:
        steps = jax.random.uniform(jax.random.fold_in(jax.random.fold_in(own_key, 6), dim), (blocks,), jnp.float32, low / len(shards), largest / len(shards))
        gain = gain * jnp.repeat(jnp.exp(steps), dims[dim] // blocks).reshape((-1,) + (1,) * (len(dims) - 1 - dim))
    return gain


def scatter_about(stream_key, shape, deviation, bound, shards=(), held_as=jnp.bfloat16):
    loudness = levels(stream_key, shape, shards, -0.22, 0.18) if shards else 1.0
    drawn = jax.random.normal(stream_key, shape, jnp.float32) * deviation * loudness
    return jnp.minimum(jnp.maximum(drawn, -bound), bound).astype(held_as)


def setup_inputs(seed: int = 0) -> dict:
    arg_keys = jax.random.split(jax.random.key(seed), 7)
    return {
        "right_side": draw_right_side(jax.random.fold_in(arg_keys[6], 71), 0),
        "diag_term": jnp.clip(jnp.exp(math.log(8.0) - 1.1631508 * jax.random.uniform(arg_keys[1], (NCLUST, CL), jnp.float32) ** levels(arg_keys[1], (NCLUST, CL), ((0, 128),), -0.2, 0.2)), 2.5, 8.0),
        "near_pairs": draw_near_pairs(jax.random.fold_in(arg_keys[6], 71), 0),
        "near_tiles": scatter_about(arg_keys[3], (NNEAR, CL, CL), (96 * CL) ** -0.5, 0.0390625, ((0, 128),)),
        "far_pairs": draw_far_pairs(jax.random.fold_in(arg_keys[6], 71), 0),
        "far_factors": scatter_about(arg_keys[5], (NFAR, 2, RK, CL), (32 * CL) ** -0.5, 0.0625, ((0, 128),)),
    }


def bf16_round(values):
    return lax.optimization_barrier(values.astype(jnp.bfloat16)).astype(jnp.float32)


def near_terms(summed, rounded, pair_list, tile_store):
    slot_total = tile_store.shape[0]
    block_size = math.gcd(slot_total, 256)
    block_count = slot_total // block_size
    pair_blocks = jnp.transpose(pair_list.reshape(3, block_count, block_size), (1, 0, 2))
    tile_blocks = tile_store.reshape(block_count, block_size, CL, CL)

    def near_step(acc, block_item):
        pair_block, tile_block = block_item
        row_ids = pair_block[0].astype(jnp.int32)
        col_ids = pair_block[1].astype(jnp.int32)
        live_flag = pair_block[2].astype(jnp.float32)[:, None, None]
        tiles32 = tile_block.astype(jnp.float32)
        from_col = rounded[col_ids]
        from_row = rounded[row_ids]
        to_row = jnp.einsum('bnj,bij->bni', from_col, tiles32) * live_flag
        to_col = jnp.einsum('bni,bij->bnj', from_row, tiles32) * live_flag
        acc = acc.at[row_ids].add(to_row).at[col_ids].add(to_col)
        return acc, None

    summed, unused = lax.scan(near_step, summed, (pair_blocks, tile_blocks))
    return summed


def far_terms(summed, rounded, pair_list, factor_store):
    slot_total = factor_store.shape[0]
    block_size = math.gcd(slot_total, 256)
    block_count = slot_total // block_size
    pair_blocks = jnp.transpose(pair_list.reshape(3, block_count, block_size), (1, 0, 2))
    factor_blocks = factor_store.reshape(block_count, block_size, 2, RK, CL)

    def far_step(acc, block_item):
        pair_block, factor_block = block_item
        row_ids = pair_block[0].astype(jnp.int32)
        col_ids = pair_block[1].astype(jnp.int32)
        live_flag = pair_block[2].astype(jnp.float32)[:, None, None]
        left_basis = factor_block[:, 0].astype(jnp.float32)
        right_basis = factor_block[:, 1].astype(jnp.float32)
        from_col = rounded[col_ids]
        from_row = rounded[row_ids]
        inner_part = bf16_round(jnp.einsum('bnj,bkj->bnk', from_col, right_basis))
        to_row = jnp.einsum('bnk,bki->bni', inner_part, left_basis) * live_flag
        outer_part = bf16_round(jnp.einsum('bni,bki->bnk', from_row, left_basis))
        to_col = jnp.einsum('bnk,bkj->bnj', outer_part, right_basis) * live_flag
        acc = acc.at[row_ids].add(to_row).at[col_ids].add(to_col)
        return acc, None

    summed, unused = lax.scan(far_step, summed, (pair_blocks, factor_blocks))
    return summed


def apply_operator(direction, diag_term, near_pairs, near_tiles, far_pairs, far_factors):
    rounded = bf16_round(direction)
    summed = jnp.zeros(direction.shape, jnp.float32)
    summed = near_terms(summed, rounded, near_pairs, near_tiles)
    summed = far_terms(summed, rounded, far_pairs, far_factors)
    return diag_term[:, None, :] * direction + summed


def reference(right_side, diag_term, near_pairs, near_tiles, far_pairs, far_factors):
    solution_field = jnp.zeros_like(right_side)
    residual = right_side
    direction = right_side
    norm_now = jnp.sum(residual * residual, axis=(0, 2))
    for iteration in range(ITERS):
        image_field = apply_operator(direction, diag_term, near_pairs, near_tiles, far_pairs, far_factors)
        step_size = norm_now / jnp.sum(direction * image_field, axis=(0, 2))
        solution_field = solution_field + step_size[None, :, None] * direction
        residual = residual - step_size[None, :, None] * image_field
        norm_next = jnp.sum(residual * residual, axis=(0, 2))
        direction = residual + (norm_next / norm_now)[None, :, None] * direction
        norm_now = norm_next
    return solution_field, residual
```

```python
import functools

import jax
import jax.numpy as jnp
from jax import lax
from jax.experimental import pallas as pl
from jax.experimental.pallas import tpu as pltpu
from jax.sharding import PartitionSpec as P

ITERS = 3
MESH = pl.DeviceIdType.MESH
NEAR_UNROLL = 16
FAR_UNROLL = 6
F32 = jnp.float32
BF16 = jnp.bfloat16

XO_Z = 0
XO_SIB = 3
XN_ROW = 7
XN_SIB = 11
PR_NEXT = 15
PR_OWN = 16
RN = 17
RO = 21
AR_COL = 24
AR_ROW = 31
N_SEM = 46


def sorted_tables(key, source, dummy):
    count = key.shape[0]
    ids = jnp.arange(count, dtype=jnp.int32)
    before = (key[None, :] < key[:, None]) | ((key[None, :] == key[:, None]) & (ids[None, :] < ids[:, None]))
    rank = jnp.sum(before.astype(jnp.int32), axis=1)
    hit = (rank[:, None] == ids[None, :]).astype(jnp.int32)
    slot = jnp.sum(hit * ids[:, None], axis=0)
    src = jnp.sum(hit * source[:, None], axis=0)
    skey = jnp.sum(hit * key[:, None], axis=0)
    places = jnp.arange(64, dtype=jnp.int32)
    upto = jnp.sum((key[:, None] <= places[None, :]).astype(jnp.int32), axis=0)
    equal = jnp.sum((key[:, None] == places[None, :]).astype(jnp.int32), axis=0)
    last = jnp.where(equal > 0, upto - 1, dummy)
    pad = lambda v: jnp.pad(v, (0, 128 - v.shape[0]))
    return [pad(slot), pad(src), pad(skey), pad(last)]


def make_tables(near_pairs, far_pairs, offset):
    rows = []
    for pairs in (near_pairs, far_pairs):
        count = pairs.shape[1]
        row = jnp.clip(pairs[0] - offset, 0, 31)
        col = jnp.clip(pairs[1] - offset, 0, 63)
        live = pairs[2] != 0
        rows += sorted_tables(jnp.where(live, col, 64), row, count)
        rows += sorted_tables(jnp.where(live, row, 64), col, count)
    return jnp.stack(rows)


def kernel(
    tab, b_ref, diag_ref, tiles_hbm, fac_hbm, x_ref, r_ref,
    tiles, fac, pn, pf, xo, xn, ext, acc1, stn, sto, prn, pro, zsn, zso, rn, ro, ar1, ar2,
    p_ref, q_ref, gd, sc, ss, rs, ls,
):
    g = lax.axis_index("row")
    me = lax.axis_index("col")
    n_row = lax.axis_size("row")
    n_col = lax.axis_size("col")
    z, core = me // 2, me % 2
    n_z = n_col // 2
    sib = z * 2 + (1 - core)
    nxt, prv = (g + 1) % n_row, (g + n_row - 1) % n_row
    k_near = tiles.shape[0]
    k_far = fac.shape[0]

    def zc(d):
        return ((z + d + n_z) % n_z) * 2 + core

    def zs(d):
        return ((z + d + n_z) % n_z) * 2 + (1 - core)

    def rdma(it, idx, src, dst, row, col):
        return pltpu.make_async_remote_copy(
            src_ref=src, dst_ref=dst, send_sem=ss.at[it, idx], recv_sem=rs.at[it, idx],
            device_id=(row, col), device_id_type=MESH,
        )

    def shard(ref, it, col):
        return ref.at[it, pl.ds(col * 4, 4)]

    load_tiles = pltpu.make_async_copy(tiles_hbm, tiles, ls.at[0])
    load_fac = pltpu.make_async_copy(fac_hbm, fac, ls.at[1])
    load_tiles.start()
    load_fac.start()

    barrier = pltpu.get_barrier_semaphore()
    peers = [(g, (me + k) % n_col) for k in range(1, n_col)]
    peers += [((g + k) % n_row, me) for k in range(1, n_row)]
    peers += [(nxt, zc(d)) for d in range(1, n_z)] + [(prv, zc(d)) for d in range(1, n_z)]
    for peer in peers:
        pl.semaphore_signal(barrier, inc=1, device_id=peer, device_id_type=MESH)

    sub = lax.broadcasted_iota(jnp.int32, (32, 128), 0)
    lane = lax.broadcasted_iota(jnp.int32, (32, 128), 1)

    def lane_sum(field):
        return jnp.sum(field[:, :128] + field[:, 128:], axis=1, keepdims=True)

    def to_row(cols):
        total = jnp.zeros((32, 128), F32)
        for j, col in enumerate(cols):
            total += jnp.where(lane == sub + 32 * j, col, 0.0)
        return jnp.sum(total, axis=0, keepdims=True)

    def to_col(row, j):
        return jnp.sum(jnp.where(lane == sub + 32 * j, row, 0.0), axis=1, keepdims=True)

    def wide(col):
        return jnp.broadcast_to(col, (32, 128))

    total = jnp.zeros((32, 256), F32)
    for j in range(4):
        r = b_ref[j]
        r_ref[j] = r
        x_ref[j] = jnp.zeros((32, 256), F32)
        p_ref[j] = jnp.zeros((32, 256), F32)
        q_ref[j] = jnp.zeros((32, 256), F32)
        xo[0, me * 4 + j] = r.astype(BF16)
        total += r * r
    gd[0] = wide(lane_sum(total))
    gd[1] = jnp.zeros((32, 128), F32)
    sc[0] = jnp.ones((32, 128), F32)
    sc[1] = jnp.zeros((32, 128), F32)
    pn[k_near] = jnp.zeros((32, 256), F32)
    pf[k_far] = jnp.zeros((32, 256), F32)

    pl.semaphore_wait(barrier, len(peers))

    def first_sends(it):
        mine = shard(xo, it, me)
        return [
            rdma(it, XO_Z + d - 1, mine, mine, g, zc(d)) for d in (1, 3, 2)
        ] + [
            rdma(it, XO_SIB, mine, mine, g, sib),
            rdma(it, XN_ROW, mine, shard(xn, it, me), prv, me),
        ]

    def from_z(it, d):
        here = shard(xo, it, zc(-d))
        return rdma(it, XO_Z + d - 1, here, here, g, zc(d))

    def relays(it, d):
        here = shard(xo, it, zc(-d))
        return [
            rdma(it, XO_SIB + d, here, here, g, sib),
            rdma(it, XN_ROW + d, here, shard(xn, it, zc(-d)), prv, me),
        ]

    def from_sib(it, d):
        here = shard(xo, it, zs(-d))
        return rdma(it, XO_SIB + d, here, here, g, sib)

    def next_from_row(it, d):
        here = shard(xn, it, zc(-d))
        return rdma(it, XN_ROW + d, here, here, prv, me)

    def next_to_sib(it, d):
        here = shard(xn, it, zc(-d))
        return rdma(it, XN_SIB + d, here, here, g, sib)

    def next_from_sib(it, d):
        here = shard(xn, it, zs(-d))
        return rdma(it, XN_SIB + d, here, here, g, sib)

    def pair_next(it):
        return rdma(it, PR_NEXT, stn.at[it, 1 - core], prn.at[it], g, sib)

    def pair_own(it):
        return rdma(it, PR_OWN, sto.at[it, 1 - core], pro.at[it], g, sib)

    def terms_next(it, d):
        return rdma(it, RN + d, zsn.at[it, (z + d) % n_z], rn.at[it, d], nxt, zc(d))

    def terms_own(it, d):
        return rdma(it, RO + d - 1, zso.at[it, (z + d) % n_z], ro.at[it, d - 1], g, zc(d))

    def dots_col(it, k):
        return rdma(it, AR_COL + k - 1, ar1.at[it, me], ar1.at[it, me], g, (me + k) % n_col)

    def dots_col_in(it, k):
        here = ar1.at[it, (me + n_col - k) % n_col]
        return rdma(it, AR_COL + k - 1, here, here, g, (me + k) % n_col)

    def dots_row(it, k):
        return rdma(it, AR_ROW + k - 1, ar2.at[it, g], ar2.at[it, g], (g + k) % n_row, me)

    def dots_row_in(it, k):
        here = ar2.at[it, (g + n_row - k) % n_row]
        return rdma(it, AR_ROW + k - 1, here, here, (g + k) % n_row, me)

    def near_phase(base, transposed):
        def step(block, acc):
            for u in range(NEAR_UNROLL):
                k = block * NEAR_UNROLL + u
                field = ext[tab[base + 1, k]]
                tile = tiles[tab[base, k]]
                keep = (tab[base + 2, k] == tab[base + 2, lax.max(k - 1, 0)]).astype(F32)
                term = lax.dot_general(
                    field, tile, (((1,), (1 if transposed else 0,)), ((), ())),
                    preferred_element_type=F32,
                )
                acc = acc * keep + term
                pn[k] = acc
            return acc

        lax.fori_loop(0, k_near // NEAR_UNROLL, step, jnp.zeros((32, 256), F32))

    def far_phase(base, first, second):
        lanes = lax.broadcasted_iota(jnp.int32, (256, 256), 1) // 32
        rows = lax.broadcasted_iota(jnp.int32, (256, 256), 0) // 32
        mask = lanes == rows

        def step(block, acc):
            for u in range(FAR_UNROLL):
                start = (block * FAR_UNROLL + u) * 8
                fields, lefts, rights = [], [], []
                for q in range(8):
                    slot = tab[base, start + q]
                    fields.append(ext[tab[base + 1, start + q]])
                    lefts.append(fac[slot, first])
                    rights.append(fac[slot, second])
                field = jnp.concatenate(fields, axis=0)
                left = jnp.concatenate(lefts, axis=0)
                right = jnp.concatenate(rights, axis=0)
                inner = lax.dot_general(field, left, (((1,), (1,)), ((), ())), preferred_element_type=F32)
                inner = jnp.where(mask, inner, 0.0).astype(BF16)
                term = lax.dot_general(inner, right, (((1,), (0,)), ((), ())), preferred_element_type=F32)
                for q in range(8):
                    k = start + q
                    keep = (tab[base + 2, k] == tab[base + 2, lax.max(k - 1, 0)]).astype(F32)
                    acc = acc * keep + term[q * 32 : q * 32 + 32]
                    pf[k] = acc
            return acc

        lax.fori_loop(0, k_far // (8 * FAR_UNROLL), step, jnp.zeros((32, 256), F32))

    for copy in first_sends(0):
        copy.start()
    load_tiles.wait()
    load_fac.wait()

    def iteration(it, carry):
        for d in (1, 3, 2):
            from_z(it, d).wait_recv()
            for copy in relays(it, d):
                copy.start()
        next_from_row(it, 0).wait_recv()
        next_to_sib(it, 0).start()
        for d in (0, 1, 3, 2):
            from_sib(it, d).wait_recv()
        ext[pl.ds(0, 32)] = xo[it]

        near_phase(0, False)
        for d in (1, 3):
            next_from_row(it, d).wait_recv()
            next_to_sib(it, d).start()
        far_phase(8, 0, 1)
        next_from_row(it, 2).wait_recv()
        next_to_sib(it, 2).start()
        for d in (0, 1, 3, 2):
            next_from_sib(it, d).wait_recv()
        ext[pl.ds(32, 32)] = xn[it]

        def fold_next(chunk, total):
            for c in range(2):
                for j in range(4):
                    place = chunk * 8 + c * 4 + j + 32
                    out = pn[tab[3, place]] + pf[tab[11, place]]
                    stn[it, c, chunk, j] = out.astype(BF16)
                    total += out * ext[place].astype(F32)
            return total

        total = lax.fori_loop(0, 4, fold_next, jnp.zeros((32, 256), F32))
        pair_next(it).start()

        def fold_own(chunk, total):
            for i in range(8):
                place = chunk * 8 + i
                out = pn[tab[3, place]] + pf[tab[11, place]]
                acc1[place] = out
                total += out * ext[place].astype(F32)
            return total

        total = lax.fori_loop(0, 4, fold_own, total)
        total = total * 2.0
        for j in range(4):
            r = r_ref[j]
            total += (diag_ref[pl.ds(j, 1), :] * r) * r
        ar1[it, me] = jnp.broadcast_to(to_row([lane_sum(total), gd[0], gd[1]]), (8, 128))
        for k in range(1, 8):
            dots_col(it, k).start()

        near_phase(4, True)

        pair_next(it).wait_recv()
        for chunk in range(4):
            for j in range(4):
                zsn[it, chunk, j] = (
                    stn[it, core, chunk, j].astype(F32) + prn[it, chunk, j].astype(F32)
                ).astype(BF16)
        for d in (1, 3, 2, 0):
            terms_next(it, d).start()
        row = jnp.zeros((8, 128), F32)
        for k in range(1, 8):
            dots_col_in(it, k).wait_recv()
        for k in range(8):
            row += ar1[it, k]
        ar2[it, g] = row
        for k in range(1, 16):
            dots_row(it, k).start()

        far_phase(12, 1, 0)

        def fold_rows(chunk, carry):
            for c in range(2):
                for j in range(4):
                    place = chunk * 8 + c * 4 + j
                    out = acc1[place] + (pn[tab[7, place]] + pf[tab[15, place]])
                    sto[it, c, chunk, j] = out.astype(BF16)
            return carry

        lax.fori_loop(0, 4, fold_rows, 0)
        pair_own(it).start()
        pair_own(it).wait_recv()
        for chunk in range(4):
            for j in range(4):
                zso[it, chunk, j] = (
                    sto[it, core, chunk, j].astype(F32) + pro[it, chunk, j].astype(F32)
                ).astype(BF16)
        for d in (1, 3, 2):
            terms_own(it, d).start()

        row = jnp.zeros((8, 128), F32)
        for k in range(1, 16):
            dots_row_in(it, k).wait_recv()
        for k in range(16):
            row += ar2[it, k]
        row = row[:1]
        delta, gamma, eta = to_col(row, 0), to_col(row, 1), to_col(row, 2)
        beta = gamma / sc[0][:, :1]
        curvature = delta + 2.0 * beta * eta + beta * beta * sc[1][:, :1]
        alpha = gamma / curvature
        sc[0] = wide(gamma)
        sc[1] = wide(curvature)

        for d in range(4):
            terms_next(it, d).wait_recv()
        for d in range(1, 4):
            terms_own(it, d).wait_recv()
        total = jnp.zeros((32, 256), F32)
        cross = jnp.zeros((32, 256), F32)
        for j in range(4):
            r = r_ref[j]
            w = diag_ref[pl.ds(j, 1), :] * r
            w += sto[it, core, z, j].astype(F32) + pro[it, z, j].astype(F32)
            for d in range(4):
                w += rn[it, d, j].astype(F32)
            for d in range(3):
                w += ro[it, d, j].astype(F32)
            p = r + beta * p_ref[j]
            q = w + beta * q_ref[j]
            p_ref[j] = p
            q_ref[j] = q
            x_ref[j] = x_ref[j] + alpha * p
            r = r - alpha * q
            r_ref[j] = r

            @pl.when(it < ITERS - 1)
            def _():
                xo[lax.min(it + 1, ITERS - 1), me * 4 + j] = r.astype(BF16)

            total += r * r
            cross += r * q

        @pl.when(it < ITERS - 1)
        def _():
            for copy in first_sends(it + 1):
                copy.start()

        gd[0] = wide(lane_sum(total))
        gd[1] = wide(lane_sum(cross))
        return carry

    lax.fori_loop(0, ITERS, iteration, 0)

    def drain(it, carry):
        for copy in first_sends(it):
            copy.wait_send()
        for d in (1, 2, 3):
            for copy in relays(it, d):
                copy.wait_send()
            terms_own(it, d).wait_send()
        for d in range(4):
            next_to_sib(it, d).wait_send()
            terms_next(it, d).wait_send()
        pair_next(it).wait_send()
        pair_own(it).wait_send()
        for k in range(1, 8):
            dots_col(it, k).wait_send()
        for k in range(1, 16):
            dots_row(it, k).wait_send()
        return carry

    lax.fori_loop(0, ITERS, drain, 0)


def body(right_side, diag_term, near_pairs, near_tiles, far_pairs, far_factors):
    offset = lax.axis_index("row") * 32
    tables = make_tables(near_pairs, far_pairs, offset)
    k_near, k_far = near_tiles.shape[0], far_factors.shape[0]
    field = jax.ShapeDtypeStruct((4, 32, 256), F32)
    vmem = pl.BlockSpec(memory_space=pltpu.VMEM)
    hbm = pl.BlockSpec(memory_space=pl.ANY)
    return pl.pallas_call(
        kernel,
        out_shape=(field, field),
        in_specs=[pl.BlockSpec(memory_space=pltpu.SMEM), vmem, vmem, hbm, hbm],
        out_specs=(vmem, vmem),
        scratch_shapes=[
            pltpu.VMEM((k_near, 256, 256), BF16),
            pltpu.VMEM((k_far, 2, 32, 256), BF16),
            pltpu.VMEM((k_near + 1, 32, 256), F32),
            pltpu.VMEM((k_far + 1, 32, 256), F32),
            pltpu.VMEM((ITERS, 32, 32, 256), BF16),
            pltpu.VMEM((ITERS, 32, 32, 256), BF16),
            pltpu.VMEM((64, 32, 256), BF16),
            pltpu.VMEM((32, 32, 256), F32),
            pltpu.VMEM((ITERS, 2, 4, 4, 32, 256), BF16),
            pltpu.VMEM((ITERS, 2, 4, 4, 32, 256), BF16),
            pltpu.VMEM((ITERS, 4, 4, 32, 256), BF16),
            pltpu.VMEM((ITERS, 4, 4, 32, 256), BF16),
            pltpu.VMEM((ITERS, 4, 4, 32, 256), BF16),
            pltpu.VMEM((ITERS, 4, 4, 32, 256), BF16),
            pltpu.VMEM((ITERS, 4, 4, 32, 256), BF16),
            pltpu.VMEM((ITERS, 3, 4, 32, 256), BF16),
            pltpu.VMEM((ITERS, 8, 8, 128), F32),
            pltpu.VMEM((ITERS, 16, 8, 128), F32),
            pltpu.VMEM((4, 32, 256), F32),
            pltpu.VMEM((4, 32, 256), F32),
            pltpu.VMEM((2, 32, 128), F32),
            pltpu.VMEM((2, 32, 128), F32),
            pltpu.SemaphoreType.DMA((ITERS, N_SEM)),
            pltpu.SemaphoreType.DMA((ITERS, N_SEM)),
            pltpu.SemaphoreType.DMA((2,)),
        ],
        compiler_params=pltpu.CompilerParams(
            collective_id=0, has_side_effects=True, vmem_limit_bytes=60 * 2**20
        ),
    )(tables, right_side, diag_term, near_tiles, far_factors)


def solution(mesh):
    placed = (
        P(("row", "col"), None, None),
        P(("row", "col"), None),
        P(None, ("row", "col")),
        P(("row", "col"), None, None),
        P(None, ("row", "col")),
        P(("row", "col"), None, None, None),
    )
    return jax.shard_map(
        body,
        mesh=mesh,
        in_specs=placed,
        out_specs=(P(("row", "col"), None, None), P(("row", "col"), None, None)),
        check_vma=False,
    )
```

```python
import functools

import jax
import jax.numpy as jnp
from jax import lax
from jax.experimental import pallas as pl
from jax.experimental.pallas import tpu as pltpu
from jax.sharding import PartitionSpec as P

ITERS = 3
MESH = pl.DeviceIdType.MESH
NEAR_UNROLL = 32
FAR_UNROLL = 12
F32 = jnp.float32
BF16 = jnp.bfloat16

XO_Z = 0
XO_SIB = 3
XN_ROW = 7
XN_SIB = 11
PR_NEXT = 15
PR_OWN = 16
RNZ = 17
RN = 20
RF = 46
RO = 21
AR_COL = 24
AR_ROW = 31
N_SEM = 47


def sorted_tables(key, source, dummy):
    sub = lax.broadcasted_iota(jnp.int32, (128, 128), 0)
    lane = lax.broadcasted_iota(jnp.int32, (128, 128), 1)
    eye = sub == lane
    packed = key + 128 * source + 16384 * lane[:1]
    column = jnp.sum(jnp.where(eye, packed, 0), axis=1, keepdims=True)
    key_col = column & 127
    before = (key < key_col) | ((key == key_col) & (lane < sub))
    rank = jnp.sum(before.astype(jnp.int32), axis=1, keepdims=True)
    ordered = jnp.sum(jnp.where(rank == lane, column, 0), axis=0, keepdims=True)
    upto = jnp.sum((key_col <= lane).astype(jnp.int32), axis=0, keepdims=True)
    equal = jnp.sum((key_col == lane).astype(jnp.int32), axis=0, keepdims=True)
    last = jnp.where(equal > 0, upto - 1, dummy)
    return [ordered >> 14, (ordered >> 7) & 127, ordered & 127, last]


def kernel(
    b_ref, diag_ref, near_pairs, far_pairs, tiles_hbm, fac_hbm, x_ref, r_ref,
    tiles, turned, fac, pn, pf, pn2, pf2, xo, xn, ext, acc1, stn, sto, prn, pro, zsn, zso, rnz, xs, rn, rf, ro, ar1, ar2,
    p_ref, q_ref, gd, sc, pairs, tabv, tab, ss, rs, ls,
):
    g = lax.axis_index("row")
    me = lax.axis_index("col")
    n_row = lax.axis_size("row")
    n_col = lax.axis_size("col")
    z, core = me // 2, lax.rem(me, 2)
    n_z = n_col // 2
    sib = z * 2 + (1 - core)
    nxt, prv = lax.rem(g + 1, n_row), lax.rem(g + n_row - 1, n_row)
    at_z = [lax.rem(z + d, n_z) for d in range(n_z)]
    at_col = [lax.rem(me + k, n_col) for k in range(n_col)]
    at_row = [lax.rem(g + k, n_row) for k in range(n_row)]
    k_near = tiles.shape[0]
    k_far = fac.shape[0]

    def zc(d):
        return at_z[d % n_z] * 2 + core

    def zs(d):
        return at_z[d % n_z] * 2 + (1 - core)

    def rdma(it, idx, src, dst, row, col):
        return pltpu.make_async_remote_copy(
            src_ref=src, dst_ref=dst, send_sem=ss.at[it, idx], recv_sem=rs.at[it, idx],
            device_id=(row, col), device_id_type=MESH,
        )

    def shard(ref, it, col):
        return ref.at[it, pl.ds(col * 4, 4)]

    load_tiles = pltpu.make_async_copy(tiles_hbm, tiles, ls.at[0])
    load_fac = pltpu.make_async_copy(fac_hbm, fac, ls.at[1])
    load_tiles.start()
    load_fac.start()

    barrier = pltpu.get_barrier_semaphore()
    peers = [(g, at_col[k]) for k in range(1, n_col)]
    peers += [(at_row[k], me) for k in range(1, n_row)]
    for peer in peers:
        pl.semaphore_signal(barrier, inc=1, device_id=peer, device_id_type=MESH)

    sub = lax.broadcasted_iota(jnp.int32, (32, 128), 0)
    lane = lax.broadcasted_iota(jnp.int32, (32, 128), 1)

    def lane_sum(field):
        return jnp.sum(field[:, :128] + field[:, 128:], axis=1, keepdims=True)

    def to_row(cols):
        total = jnp.zeros((32, 128), F32)
        for j, col in enumerate(cols):
            total += jnp.where(lane == sub + 32 * j, col, 0.0)
        return jnp.sum(total, axis=0, keepdims=True)

    def to_col(row, j):
        return jnp.sum(jnp.where(lane == sub + 32 * j, row, 0.0), axis=1, keepdims=True)

    def wide(col):
        return jnp.broadcast_to(col, (32, 128))

    total = jnp.zeros((32, 256), F32)
    for j in range(4):
        r = b_ref[j]
        r_ref[j] = r
        x_ref[j] = jnp.zeros((32, 256), F32)
        p_ref[j] = jnp.zeros((32, 256), F32)
        q_ref[j] = jnp.zeros((32, 256), F32)
        xo[0, me * 4 + j] = r.astype(BF16)
        total += r * r
    gd[0] = wide(lane_sum(total))
    gd[1] = jnp.zeros((32, 128), F32)
    sc[0] = jnp.ones((32, 128), F32)
    sc[1] = jnp.zeros((32, 128), F32)
    for ref in (pn, pn2):
        ref[k_near] = jnp.zeros((32, 256), F32)
    for ref in (pf, pf2):
        ref[k_far] = jnp.zeros((32, 256), F32)

    pairs[...] = jnp.zeros((8, 128), jnp.int32)
    pairs[pl.ds(0, 3), pl.ds(0, k_near)] = near_pairs[...]
    pairs[pl.ds(3, 3), pl.ds(0, k_far)] = far_pairs[...]
    tables = []
    for first, count in ((0, k_near), (3, k_far)):
        row_id = jnp.clip(pairs[pl.ds(first, 1), :] - g * 32, 0, 31)
        col_id = jnp.clip(pairs[pl.ds(first + 1, 1), :] - g * 32, 0, 63)
        live = pairs[pl.ds(first + 2, 1), :] != 0
        tables += sorted_tables(jnp.where(live, col_id, 64), row_id, count)
        tables += sorted_tables(jnp.where(live, row_id, 64), col_id, count)
    for i, line in enumerate(tables):
        tabv[pl.ds(i, 1), :] = line
    copy_tab = pltpu.make_async_copy(tabv, tab, ls.at[2])
    copy_tab.start()

    pl.semaphore_wait(barrier, len(peers))

    def first_sends(it):
        mine = shard(xo, it, me)
        return [
            rdma(it, XO_Z + d - 1, mine, mine, g, zc(d)) for d in (1, 3, 2)
        ] + [
            rdma(it, XO_SIB, mine, mine, g, sib),
            rdma(it, XN_ROW, mine, shard(xn, it, me), prv, me),
        ]

    def from_z(it, d):
        here = shard(xo, it, zc(-d))
        return rdma(it, XO_Z + d - 1, here, here, g, zc(d))

    def relays(it, d):
        here = shard(xo, it, zc(-d))
        copies = [rdma(it, XO_SIB + d, here, here, g, sib)]
        if d == 2:
            copies.append(rdma(it, XN_ROW + d, here, shard(xn, it, zc(-d)), prv, me))
        return copies

    def next_to_z(it, d):
        here = shard(xn, it, me)
        return rdma(it, XN_ROW + d, here, here, g, zc(d))

    def from_sib(it, d):
        here = shard(xo, it, zs(-d))
        return rdma(it, XO_SIB + d, here, here, g, sib)

    def next_from_row(it, d):
        here = shard(xn, it, zc(-d))
        return rdma(it, XN_ROW + d, here, here, prv, me)

    def next_to_sib(it, d):
        here = shard(xn, it, zc(-d))
        return rdma(it, XN_SIB + d, here, here, g, sib)

    def next_from_sib(it, d):
        here = shard(xn, it, zs(-d))
        return rdma(it, XN_SIB + d, here, here, g, sib)

    def pair_next(it):
        return rdma(it, PR_NEXT, stn.at[it, 1 - core], prn.at[it], g, sib)

    def pair_own(it):
        return rdma(it, PR_OWN, sto.at[it, 1 - core], pro.at[it], g, sib)

    def terms_next(it, d):
        return rdma(it, RNZ + d - 1, zsn.at[it, d - 1], rnz.at[it, d - 1], g, zc(d))

    def terms_far(it):
        return rdma(it, RF, zsn.at[it, 1], rf.at[it], nxt, me)

    def terms_over(it):
        return rdma(it, RN, xs.at[it], rn.at[it], nxt, me)

    def terms_own(it, d):
        return rdma(it, RO + d - 1, zso.at[it, d - 1], ro.at[it, d - 1], g, zc(d))

    def dots_col(it, k):
        return rdma(it, AR_COL + k - 1, ar1.at[it, me], ar1.at[it, me], g, at_col[k])

    def dots_col_in(it, k):
        here = ar1.at[it, at_col[n_col - k]]
        return rdma(it, AR_COL + k - 1, here, here, g, at_col[k])

    def dots_row(it, k):
        return rdma(it, AR_ROW + k - 1, ar2.at[it, g], ar2.at[it, g], at_row[k], me)

    def dots_row_in(it, k):
        here = ar2.at[it, at_row[n_row - k]]
        return rdma(it, AR_ROW + k - 1, here, here, at_row[k], me)

    def near_phase(base, blocks, sums, first, last, acc):
        def step(block, acc):
            for u in range(NEAR_UNROLL):
                k = block * NEAR_UNROLL + u
                field = ext[tab[base + 1, k]]
                tile = blocks[tab[base, k]]
                keep = (tab[base + 2, k] == tab[base + 2, lax.max(k - 1, 0)]).astype(F32)
                term = lax.dot_general(field, tile, (((1,), (0,)), ((), ())), preferred_element_type=F32)
                acc = acc * keep + term
                sums[k] = acc
            return acc

        return lax.fori_loop(first // NEAR_UNROLL, last // NEAR_UNROLL, step, acc)

    def far_phase(base, first, second, sums):
        lanes = lax.broadcasted_iota(jnp.int32, (256, 256), 1) // 32
        rows = lax.broadcasted_iota(jnp.int32, (256, 256), 0) // 32
        mask = lanes == rows

        def step(block, acc):
            for u in range(FAR_UNROLL):
                start = (block * FAR_UNROLL + u) * 8
                fields, lefts, rights = [], [], []
                for q in range(8):
                    slot = tab[base, start + q]
                    fields.append(ext[tab[base + 1, start + q]])
                    lefts.append(fac[slot, first])
                    rights.append(fac[slot, second])
                field = jnp.concatenate(fields, axis=0)
                left = jnp.concatenate(lefts, axis=0)
                right = jnp.concatenate(rights, axis=0)
                inner = lax.dot_general(field, left, (((1,), (1,)), ((), ())), preferred_element_type=F32)
                inner = jnp.where(mask, inner, 0.0).astype(BF16)
                term = lax.dot_general(inner, right, (((1,), (0,)), ((), ())), preferred_element_type=F32)
                for q in range(8):
                    k = start + q
                    keep = (tab[base + 2, k] == tab[base + 2, lax.max(k - 1, 0)]).astype(F32)
                    acc = acc * keep + term[q * 32 : q * 32 + 32]
                    sums[k] = acc
            return acc

        lax.fori_loop(0, k_far // (8 * FAR_UNROLL), step, jnp.zeros((32, 256), F32))

    for copy in first_sends(0):
        copy.start()
    copy_tab.wait()
    load_tiles.wait()

    def turn(block, carry):
        for u in range(4):
            turned[block * 4 + u] = tiles[block * 4 + u].T
        return carry

    lax.fori_loop(0, k_near // 4, turn, 0)
    load_fac.wait()

    def iteration(it, carry):
        for d in (1, 3):
            from_z(it, d).wait_recv()
            for copy in relays(it, d):
                copy.start()
        next_from_row(it, 0).wait_recv()
        for d in (1, 3):
            next_to_z(it, d).start()
        from_z(it, 2).wait_recv()
        for copy in relays(it, 2):
            copy.start()
        next_to_sib(it, 0).start()
        for d in (0, 1, 3, 2):
            from_sib(it, d).wait_recv()
        ext[pl.ds(0, 32)] = xo[it]

        zero = jnp.zeros((32, 256), F32)
        far_phase(8, 0, 1, pf)
        acc = near_phase(0, tiles, pn, 0, k_near // 2, zero)
        for d in (1, 3, 2):
            next_from_row(it, d).wait_recv()
            next_to_sib(it, d).start()
        near_phase(0, tiles, pn, k_near // 2, k_near, acc)

        def fold_next(chunk, carry):
            for c in range(2):
                for j in range(4):
                    place = chunk * 8 + c * 4 + j + 32
                    out = pn[tab[3, place]] + pf[tab[11, place]]
                    acc1[place] = out
                    stn[it, c, chunk, j] = out.astype(BF16)
            return carry

        lax.fori_loop(0, 4, fold_next, 0)
        pair_next(it).start()

        for d in (0, 1, 3, 2):
            next_from_sib(it, d).wait_recv()
        ext[pl.ds(32, 32)] = xn[it]

        acc = near_phase(4, turned, pn2, 0, k_near // 2, zero)

        pair_next(it).wait_recv()
        for d in (2, 1, 3):
            chunk = at_z[d]
            for j in range(4):
                zsn[it, d - 1, j] = (
                    stn[it, core, chunk, j].astype(F32) + prn[it, chunk, j].astype(F32)
                ).astype(BF16)
            (terms_far(it) if d == 2 else terms_next(it, d)).start()

        def fold_own(chunk, total):
            for i in range(8):
                place = chunk * 8 + i
                out = pn[tab[3, place]] + pf[tab[11, place]]
                acc1[place] = out
                total += out * ext[place].astype(F32)
            return total

        total = lax.fori_loop(0, 4, fold_own, zero)
        def dot_next(chunk, total):
            for i in range(8):
                place = chunk * 8 + i + 32
                total += acc1[place] * ext[place].astype(F32)
            return total

        total = lax.fori_loop(0, 4, dot_next, total) * 2.0
        for j in range(4):
            r = r_ref[j]
            total += (diag_ref[pl.ds(j, 1), :] * r) * r
        ar1[it, me] = to_row([lane_sum(total), gd[0], gd[1]])
        for k in range(1, 8):
            dots_col(it, k).start()

        far_phase(12, 1, 0, pf2)
        near_phase(4, turned, pn2, k_near // 2, k_near, acc)

        def fold_rows(chunk, c):
            for j in range(4):
                place = chunk * 8 + c * 4 + j
                out = acc1[place] + (pn2[tab[7, place]] + pf2[tab[15, place]])
                sto[it, c, chunk, j] = out.astype(BF16)
            return c

        lax.fori_loop(0, 4, fold_rows, 1 - core)
        pair_own(it).start()
        lax.fori_loop(0, 4, fold_rows, core)
        row = jnp.zeros((1, 128), F32)
        for k in range(1, 8):
            dots_col_in(it, k).wait_recv()
        for k in range(8):
            row += ar1[it, k]
        ar2[it, g] = row
        for k in range(1, 16):
            dots_row(it, k).start()
        pair_own(it).wait_recv()
        for d in (1, 3, 2):
            chunk = at_z[d]
            if d == 2:
                terms_far(it).wait_recv()
            for j in range(4):
                out = sto[it, core, chunk, j].astype(F32) + pro[it, chunk, j].astype(F32)
                if d == 2:
                    out += rf[it, j].astype(F32)
                zso[it, d - 1, j] = out.astype(BF16)
            terms_own(it, d).start()

        for d in (1, 3):
            terms_next(it, d).wait_recv()
        for j in range(4):
            out = stn[it, core, z, j].astype(F32) + prn[it, z, j].astype(F32)
            for d in (0, 2):
                out += rnz[it, d, j].astype(F32)
            xs[it, j] = out.astype(BF16)
        terms_over(it).start()

        row = jnp.zeros((1, 128), F32)
        for k in range(1, 16):
            dots_row_in(it, k).wait_recv()
        for k in range(16):
            row += ar2[it, k]
        delta, gamma, eta = to_col(row, 0), to_col(row, 1), to_col(row, 2)
        beta = gamma / sc[0][:, :1]
        curvature = delta + 2.0 * beta * eta + beta * beta * sc[1][:, :1]
        alpha = gamma / curvature
        sc[0] = wide(gamma)
        sc[1] = wide(curvature)

        for j in range(4):
            r = r_ref[j]
            p = r + beta * p_ref[j]
            p_ref[j] = p
            x_ref[j] = x_ref[j] + alpha * p
            q = diag_ref[pl.ds(j, 1), :] * r + beta * q_ref[j]
            q_ref[j] = q + (sto[it, core, z, j].astype(F32) + pro[it, z, j].astype(F32))
        for d in (1, 3, 2):
            terms_own(it, d).wait_recv()
        terms_over(it).wait_recv()
        total = jnp.zeros((32, 256), F32)
        cross = jnp.zeros((32, 256), F32)
        for j in range(4):
            q = q_ref[j] + rn[it, j].astype(F32)
            for d in range(3):
                q += ro[it, d, j].astype(F32)
            q_ref[j] = q
            r = r_ref[j] - alpha * q
            r_ref[j] = r

            @pl.when(it < ITERS - 1)
            def _():
                xo[lax.min(it + 1, ITERS - 1), me * 4 + j] = r.astype(BF16)

            total += r * r
            cross += r * q

        @pl.when(it < ITERS - 1)
        def _():
            for copy in first_sends(it + 1):
                copy.start()

        gd[0] = wide(lane_sum(total))
        gd[1] = wide(lane_sum(cross))
        return carry

    lax.fori_loop(0, ITERS, iteration, 0)

    def drain(it, carry):
        for copy in first_sends(it):
            copy.wait_send()
        for d in (1, 2, 3):
            for copy in relays(it, d):
                copy.wait_send()
            terms_own(it, d).wait_send()
        for d in (1, 3):
            next_to_z(it, d).wait_send()
            terms_next(it, d).wait_send()
        terms_far(it).wait_send()
        terms_over(it).wait_send()
        for d in range(4):
            next_to_sib(it, d).wait_send()
        pair_next(it).wait_send()
        pair_own(it).wait_send()
        for k in range(1, 8):
            dots_col(it, k).wait_send()
        for k in range(1, 16):
            dots_row(it, k).wait_send()
        return carry

    lax.fori_loop(0, ITERS, drain, 0)


def body(right_side, diag_term, near_pairs, near_tiles, far_pairs, far_factors):
    k_near, k_far = near_tiles.shape[0], far_factors.shape[0]
    field = jax.ShapeDtypeStruct((4, 32, 256), F32)
    vmem = pl.BlockSpec(memory_space=pltpu.VMEM)
    hbm = pl.BlockSpec(memory_space=pl.ANY)
    xa, ra = pl.pallas_call(
        kernel,
        out_shape=(field, field),
        in_specs=[vmem, vmem, vmem, vmem, hbm, hbm],
        out_specs=(vmem, vmem),
        scratch_shapes=[
            pltpu.VMEM((k_near, 256, 256), BF16),
            pltpu.VMEM((k_near, 256, 256), BF16),
            pltpu.VMEM((k_far, 2, 32, 256), BF16),
            pltpu.VMEM((k_near + 1, 32, 256), F32),
            pltpu.VMEM((k_far + 1, 32, 256), F32),
            pltpu.VMEM((k_near + 1, 32, 256), F32),
            pltpu.VMEM((k_far + 1, 32, 256), F32),
            pltpu.VMEM((ITERS, 32, 32, 256), BF16),
            pltpu.VMEM((ITERS, 32, 32, 256), BF16),
            pltpu.VMEM((64, 32, 256), BF16),
            pltpu.VMEM((64, 32, 256), F32),
            pltpu.VMEM((ITERS, 2, 4, 4, 32, 256), BF16),
            pltpu.VMEM((ITERS, 2, 4, 4, 32, 256), BF16),
            pltpu.VMEM((ITERS, 4, 4, 32, 256), BF16),
            pltpu.VMEM((ITERS, 4, 4, 32, 256), BF16),
            pltpu.VMEM((ITERS, 3, 4, 32, 256), BF16),
            pltpu.VMEM((ITERS, 3, 4, 32, 256), BF16),
            pltpu.VMEM((ITERS, 3, 4, 32, 256), BF16),
            pltpu.VMEM((ITERS, 4, 32, 256), BF16),
            pltpu.VMEM((ITERS, 4, 32, 256), BF16),
            pltpu.VMEM((ITERS, 4, 32, 256), BF16),
            pltpu.VMEM((ITERS, 3, 4, 32, 256), BF16),
            pltpu.VMEM((ITERS, 8, 1, 128), F32),
            pltpu.VMEM((ITERS, 16, 1, 128), F32),
            pltpu.VMEM((4, 32, 256), F32),
            pltpu.VMEM((4, 32, 256), F32),
            pltpu.VMEM((2, 32, 128), F32),
            pltpu.VMEM((2, 32, 128), F32),
            pltpu.VMEM((8, 128), jnp.int32),
            pltpu.VMEM((16, 128), jnp.int32),
            pltpu.SMEM((16, 128), jnp.int32),
            pltpu.SemaphoreType.DMA((ITERS, N_SEM)),
            pltpu.SemaphoreType.DMA((ITERS, N_SEM)),
            pltpu.SemaphoreType.DMA((3,)),
        ],
        compiler_params=pltpu.CompilerParams(
            collective_id=0, has_side_effects=True, vmem_limit_bytes=60 * 2**20
        ),
    )(right_side, diag_term, near_pairs, far_pairs, near_tiles, far_factors)

    def tail(a, b, c, d):
        c[...] = a[...]
        d[...] = b[...]

    return pl.pallas_call(tail, out_shape=(field, field), in_specs=[vmem, vmem], out_specs=(vmem, vmem))(xa, ra)


def solution(mesh):
    placed = (
        P(("row", "col"), None, None),
        P(("row", "col"), None),
        P(None, ("row", "col")),
        P(("row", "col"), None, None),
        P(None, ("row", "col")),
        P(("row", "col"), None, None, None),
    )
    return jax.shard_map(
        body,
        mesh=mesh,
        in_specs=placed,
        out_specs=(P(("row", "col"), None, None), P(("row", "col"), None, None)),
        check_vma=False,
    )
```

```python
import functools

import jax
import jax.numpy as jnp
from jax import lax
from jax.experimental import pallas as pl
from jax.experimental.pallas import tpu as pltpu
from jax.sharding import PartitionSpec as P

ITERS = 3
MESH = pl.DeviceIdType.MESH
NEAR_UNROLL = 32
FAR_UNROLL = 12
F32 = jnp.float32
BF16 = jnp.bfloat16

XO_Z = 0
XO_SIB = 3
XN_ROW = 7
XN_SIB = 11
PR_NEXT = 15
PR_OWN = 16
RNZ = 17
RN = 20
RF = 46
RO = 21
AR_COL = 24
AR_ROW = 31
N_SEM = 47


def sorted_tables(key, source, dummy):
    sub = lax.broadcasted_iota(jnp.int32, (128, 128), 0)
    lane = lax.broadcasted_iota(jnp.int32, (128, 128), 1)
    eye = sub == lane
    packed = key + 128 * source + 16384 * lane[:1]
    column = jnp.sum(jnp.where(eye, packed, 0), axis=1, keepdims=True)
    key_col = column & 127
    before = (key < key_col) | ((key == key_col) & (lane < sub))
    rank = jnp.sum(before.astype(jnp.int32), axis=1, keepdims=True)
    ordered = jnp.sum(jnp.where(rank == lane, column, 0), axis=0, keepdims=True)
    upto = jnp.sum((key_col <= lane).astype(jnp.int32), axis=0, keepdims=True)
    equal = jnp.sum((key_col == lane).astype(jnp.int32), axis=0, keepdims=True)
    last = jnp.where(equal > 0, upto - 1, dummy)
    return [ordered >> 14, (ordered >> 7) & 127, ordered & 127, last]


def kernel(
    b_ref, diag_ref, near_pairs, far_pairs, tiles_hbm, fac_hbm, x_ref, r_ref,
    tiles, turned, fac, pn, pf, pn2, pf2, xo, xn, ext, acc1, stn, sto, prn, pro, zsn, zso, rnz, xs, rn, rf, ro, ar1, ar2,
    p_ref, q_ref, gd, sc, dots, pairs, tabv, tab, ss, rs, ls,
):
    g = lax.axis_index("row")
    me = lax.axis_index("col")
    n_row = lax.axis_size("row")
    n_col = lax.axis_size("col")
    z, core = me // 2, lax.rem(me, 2)
    n_z = n_col // 2
    sib = z * 2 + (1 - core)
    nxt, prv = lax.rem(g + 1, n_row), lax.rem(g + n_row - 1, n_row)
    at_z = [lax.rem(z + d, n_z) for d in range(n_z)]
    at_col = [lax.rem(me + k, n_col) for k in range(n_col)]
    at_row = [lax.rem(g + k, n_row) for k in range(n_row)]
    k_near = tiles.shape[0]
    k_far = fac.shape[0]

    def zc(d):
        return at_z[d % n_z] * 2 + core

    def zs(d):
        return at_z[d % n_z] * 2 + (1 - core)

    def rdma(it, idx, src, dst, row, col):
        return pltpu.make_async_remote_copy(
            src_ref=src, dst_ref=dst, send_sem=ss.at[it, idx], recv_sem=rs.at[it, idx],
            device_id=(row, col), device_id_type=MESH,
        )

    def shard(ref, it, col):
        return ref.at[it, pl.ds(col * 4, 4)]

    load_tiles = pltpu.make_async_copy(tiles_hbm, tiles, ls.at[0])
    load_fac = pltpu.make_async_copy(fac_hbm, fac, ls.at[1])
    load_tiles.start()
    load_fac.start()

    barrier = pltpu.get_barrier_semaphore()
    peers = [(g, at_col[k]) for k in range(1, n_col)]
    peers += [(at_row[k], me) for k in range(1, n_row)]
    for peer in peers:
        pl.semaphore_signal(barrier, inc=1, device_id=peer, device_id_type=MESH)

    sub = lax.broadcasted_iota(jnp.int32, (32, 128), 0)
    lane = lax.broadcasted_iota(jnp.int32, (32, 128), 1)

    def lane_sum(field):
        return jnp.sum(field[:, :128] + field[:, 128:], axis=1, keepdims=True)

    def to_row(cols):
        total = jnp.zeros((32, 128), F32)
        for j, col in enumerate(cols):
            total += jnp.where(lane == sub + 32 * j, col, 0.0)
        return jnp.sum(total, axis=0, keepdims=True)

    def to_col(row, j):
        return jnp.sum(jnp.where(lane == sub + 32 * j, row, 0.0), axis=1, keepdims=True)

    def wide(col):
        return jnp.broadcast_to(col, (32, 128))

    total = jnp.zeros((32, 256), F32)
    for j in range(4):
        r = b_ref[j]
        r_ref[j] = r
        x_ref[j] = jnp.zeros((32, 256), F32)
        p_ref[j] = jnp.zeros((32, 256), F32)
        q_ref[j] = jnp.zeros((32, 256), F32)
        xo[0, me * 4 + j] = r.astype(BF16)
        total += r * r
    gd[0] = wide(lane_sum(total))
    gd[1] = jnp.zeros((32, 128), F32)
    sc[0] = jnp.ones((32, 128), F32)
    sc[1] = jnp.zeros((32, 128), F32)
    for ref in (pn, pn2):
        ref[k_near] = jnp.zeros((32, 256), F32)
    for ref in (pf, pf2):
        ref[k_far] = jnp.zeros((32, 256), F32)

    pairs[...] = jnp.zeros((8, 128), jnp.int32)
    pairs[pl.ds(0, 3), pl.ds(0, k_near)] = near_pairs[...]
    pairs[pl.ds(3, 3), pl.ds(0, k_far)] = far_pairs[...]
    tables = []
    for first, count in ((0, k_near), (3, k_far)):
        row_id = jnp.clip(pairs[pl.ds(first, 1), :] - g * 32, 0, 31)
        col_id = jnp.clip(pairs[pl.ds(first + 1, 1), :] - g * 32, 0, 63)
        live = pairs[pl.ds(first + 2, 1), :] != 0
        tables += sorted_tables(jnp.where(live, col_id, 64), row_id, count)
        tables += sorted_tables(jnp.where(live, row_id, 64), col_id, count)
    for i, line in enumerate(tables):
        tabv[pl.ds(i, 1), :] = line
    copy_tab = pltpu.make_async_copy(tabv, tab, ls.at[2])
    copy_tab.start()

    pl.semaphore_wait(barrier, len(peers))

    def first_sends(it):
        mine = shard(xo, it, me)
        return [
            rdma(it, XO_Z + d - 1, mine, mine, g, zc(d)) for d in (2, 1, 3)
        ] + [
            rdma(it, XO_SIB, mine, mine, g, sib),
            rdma(it, XN_ROW, mine, shard(xn, it, me), prv, me),
        ]

    def from_z(it, d):
        here = shard(xo, it, zc(-d))
        return rdma(it, XO_Z + d - 1, here, here, g, zc(d))

    def relays(it, d):
        here = shard(xo, it, zc(-d))
        copies = [rdma(it, XO_SIB + d, here, here, g, sib)]
        if d == 2:
            copies.append(rdma(it, XN_ROW + d, here, shard(xn, it, zc(-d)), prv, me))
        return copies

    def next_to_z(it, d):
        here = shard(xn, it, me)
        return rdma(it, XN_ROW + d, here, here, g, zc(d))

    def from_sib(it, d):
        here = shard(xo, it, zs(-d))
        return rdma(it, XO_SIB + d, here, here, g, sib)

    def next_from_row(it, d):
        here = shard(xn, it, zc(-d))
        return rdma(it, XN_ROW + d, here, here, prv, me)

    def next_to_sib(it, d):
        here = shard(xn, it, zc(-d))
        return rdma(it, XN_SIB + d, here, here, g, sib)

    def next_from_sib(it, d):
        here = shard(xn, it, zs(-d))
        return rdma(it, XN_SIB + d, here, here, g, sib)

    def pair_next(it):
        return rdma(it, PR_NEXT, stn.at[it, 1 - core], prn.at[it], g, sib)

    def pair_own(it):
        return rdma(it, PR_OWN, sto.at[it, 1 - core], pro.at[it], g, sib)

    def terms_next(it, d):
        return rdma(it, RNZ + d - 1, zsn.at[it, d - 1], rnz.at[it, d - 1], g, zc(d))

    def terms_far(it):
        return rdma(it, RF, zsn.at[it, 1], rf.at[it], nxt, me)

    def terms_over(it):
        return rdma(it, RN, xs.at[it], rn.at[it], nxt, me)

    def terms_own(it, d):
        return rdma(it, RO + d - 1, zso.at[it, d - 1], ro.at[it, d - 1], g, zc(d))

    def dots_col(it, k):
        return rdma(it, AR_COL + k - 1, ar1.at[it, me], ar1.at[it, me], g, at_col[k])

    def dots_col_in(it, k):
        here = ar1.at[it, at_col[n_col - k]]
        return rdma(it, AR_COL + k - 1, here, here, g, at_col[k])

    def dots_row(it, k):
        return rdma(it, AR_ROW + k - 1, ar2.at[it, g], ar2.at[it, g], at_row[k], me)

    def dots_row_in(it, k):
        here = ar2.at[it, at_row[n_row - k]]
        return rdma(it, AR_ROW + k - 1, here, here, at_row[k], me)

    def near_phase(base, blocks, sums, first, last, acc, beside=None):
        unroll = min(NEAR_UNROLL, last - first)

        def step(block, acc):
            for u in range(unroll):
                if beside is not None:
                    beside(u)
                k = first + block * unroll + u
                field = ext[tab[base + 1, k]]
                tile = blocks[tab[base, k]]
                keep = (tab[base + 2, k] == tab[base + 2, lax.max(k - 1, 0)]).astype(F32)
                term = lax.dot_general(field, tile, (((1,), (0,)), ((), ())), preferred_element_type=F32)
                acc = acc * keep + term
                sums[k] = acc
            return acc

        return lax.fori_loop(0, (last - first) // unroll, step, acc)

    def far_phase(base, first, second, sums):
        lanes = lax.broadcasted_iota(jnp.int32, (256, 256), 1) // 32
        rows = lax.broadcasted_iota(jnp.int32, (256, 256), 0) // 32
        mask = lanes == rows

        def step(block, acc):
            for u in range(FAR_UNROLL):
                start = (block * FAR_UNROLL + u) * 8
                fields, lefts, rights = [], [], []
                for q in range(8):
                    slot = tab[base, start + q]
                    fields.append(ext[tab[base + 1, start + q]])
                    lefts.append(fac[slot, first])
                    rights.append(fac[slot, second])
                field = jnp.concatenate(fields, axis=0)
                left = jnp.concatenate(lefts, axis=0)
                right = jnp.concatenate(rights, axis=0)
                inner = lax.dot_general(field, left, (((1,), (1,)), ((), ())), preferred_element_type=F32)
                inner = jnp.where(mask, inner, 0.0).astype(BF16)
                term = lax.dot_general(inner, right, (((1,), (0,)), ((), ())), preferred_element_type=F32)
                for q in range(8):
                    k = start + q
                    keep = (tab[base + 2, k] == tab[base + 2, lax.max(k - 1, 0)]).astype(F32)
                    acc = acc * keep + term[q * 32 : q * 32 + 32]
                    sums[k] = acc
            return acc

        lax.fori_loop(0, k_far // (8 * FAR_UNROLL), step, jnp.zeros((32, 256), F32))

    for copy in first_sends(0):
        copy.start()
    copy_tab.wait()
    load_tiles.wait()

    def turn(block, carry):
        for u in range(4):
            turned[block * 4 + u] = tiles[block * 4 + u].T
        return carry

    lax.fori_loop(0, k_near // 4, turn, 0)
    load_fac.wait()

    def iteration(it, carry):
        for d in (1, 3):
            from_z(it, d).wait_recv()
            for copy in relays(it, d):
                copy.start()
        next_from_row(it, 0).wait_recv()
        for d in (1, 3):
            next_to_z(it, d).start()
        from_z(it, 2).wait_recv()
        for copy in relays(it, 2):
            copy.start()
        next_to_sib(it, 0).start()
        for d in (0, 1, 3, 2):
            from_sib(it, d).wait_recv()
        ext[pl.ds(0, 32)] = xo[it]

        zero = jnp.zeros((32, 256), F32)
        far_phase(8, 0, 1, pf)
        acc = near_phase(0, tiles, pn, 0, k_near // 2, zero)
        for d in (1, 3, 2):
            next_from_row(it, d).wait_recv()
            next_to_sib(it, d).start()
        near_phase(0, tiles, pn, k_near // 2, k_near, acc)

        def fold_next(chunk, j, c):
            place = chunk * 8 + c * 4 + j + 32
            out = pn[tab[3, place]] + pf[tab[11, place]]
            acc1[place] = out
            stn[it, c, chunk, j] = out.astype(BF16)

        for chunk in range(4):
            for j in range(4):
                fold_next(chunk, j, 1 - core)
        pair_next(it).start()

        for d in (0, 1, 3, 2):
            next_from_sib(it, d).wait_recv()
        ext[pl.ds(32, 32)] = xn[it]

        dots[...] = zero

        def fold_own(i):
            out = pn[tab[3, i]] + pf[tab[11, i]]
            acc1[i] = out
            dots[...] += out * ext[i].astype(F32) + acc1[i + 32] * ext[i + 32].astype(F32)

        acc = near_phase(4, turned, pn2, 0, 16, zero, lambda i: fold_next(i // 4, i % 4, core))

        pair_next(it).wait_recv()
        for d in (2, 1, 3):
            chunk = at_z[d]
            for j in range(4):
                zsn[it, d - 1, j] = (
                    stn[it, core, chunk, j].astype(F32) + prn[it, chunk, j].astype(F32)
                ).astype(BF16)
            (terms_far(it) if d == 2 else terms_next(it, d)).start()

        acc = near_phase(4, turned, pn2, 16, 48, acc, fold_own)
        total = dots[...] * 2.0
        for j in range(4):
            r = r_ref[j]
            total += (diag_ref[pl.ds(j, 1), :] * r) * r
        ar1[it, me] = to_row([lane_sum(total), gd[0], gd[1]])
        for k in range(1, 8):
            dots_col(it, k).start()

        far_phase(12, 1, 0, pf2)
        near_phase(4, turned, pn2, 48, k_near, acc)

        def fold_rows(chunk, c):
            for j in range(4):
                place = chunk * 8 + c * 4 + j
                out = acc1[place] + (pn2[tab[7, place]] + pf2[tab[15, place]])
                sto[it, c, chunk, j] = out.astype(BF16)
            return c

        lax.fori_loop(0, 4, fold_rows, 1 - core)
        pair_own(it).start()
        lax.fori_loop(0, 4, fold_rows, core)
        row = jnp.zeros((1, 128), F32)
        for k in range(1, 8):
            dots_col_in(it, k).wait_recv()
        for k in range(8):
            row += ar1[it, k]
        ar2[it, g] = row
        for k in range(1, 16):
            dots_row(it, k).start()
        pair_own(it).wait_recv()
        for d in (1, 3, 2):
            chunk = at_z[d]
            if d == 2:
                terms_far(it).wait_recv()
            for j in range(4):
                out = sto[it, core, chunk, j].astype(F32) + pro[it, chunk, j].astype(F32)
                if d == 2:
                    out += rf[it, j].astype(F32)
                zso[it, d - 1, j] = out.astype(BF16)
            terms_own(it, d).start()

        for d in (1, 3):
            terms_next(it, d).wait_recv()
        for j in range(4):
            out = stn[it, core, z, j].astype(F32) + prn[it, z, j].astype(F32)
            for d in (0, 2):
                out += rnz[it, d, j].astype(F32)
            xs[it, j] = out.astype(BF16)
        terms_over(it).start()

        row = jnp.zeros((1, 128), F32)
        for k in range(1, 16):
            dots_row_in(it, k).wait_recv()
        for k in range(16):
            row += ar2[it, k]
        delta, gamma, eta = to_col(row, 0), to_col(row, 1), to_col(row, 2)
        beta = gamma / sc[0][:, :1]
        curvature = delta + 2.0 * beta * eta + beta * beta * sc[1][:, :1]
        alpha = gamma / curvature
        sc[0] = wide(gamma)
        sc[1] = wide(curvature)

        for j in range(4):
            r = r_ref[j]
            p = r + beta * p_ref[j]
            p_ref[j] = p
            x_ref[j] = x_ref[j] + alpha * p
            q = diag_ref[pl.ds(j, 1), :] * r + beta * q_ref[j]
            q_ref[j] = q + (sto[it, core, z, j].astype(F32) + pro[it, z, j].astype(F32))
        for d in (1, 3, 2):
            terms_own(it, d).wait_recv()
        terms_over(it).wait_recv()
        total = jnp.zeros((32, 256), F32)
        cross = jnp.zeros((32, 256), F32)
        for j in range(4):
            q = q_ref[j] + rn[it, j].astype(F32)
            for d in range(3):
                q += ro[it, d, j].astype(F32)
            q_ref[j] = q
            r = r_ref[j] - alpha * q
            r_ref[j] = r

            @pl.when(it < ITERS - 1)
            def _():
                xo[lax.min(it + 1, ITERS - 1), me * 4 + j] = r.astype(BF16)

            total += r * r
            cross += r * q

        @pl.when(it < ITERS - 1)
        def _():
            for copy in first_sends(it + 1):
                copy.start()

        gd[0] = wide(lane_sum(total))
        gd[1] = wide(lane_sum(cross))
        return carry

    lax.fori_loop(0, ITERS, iteration, 0)

    def drain(it, carry):
        for copy in first_sends(it):
            copy.wait_send()
        for d in (1, 2, 3):
            for copy in relays(it, d):
                copy.wait_send()
            terms_own(it, d).wait_send()
        for d in (1, 3):
            next_to_z(it, d).wait_send()
            terms_next(it, d).wait_send()
        terms_far(it).wait_send()
        terms_over(it).wait_send()
        for d in range(4):
            next_to_sib(it, d).wait_send()
        pair_next(it).wait_send()
        pair_own(it).wait_send()
        for k in range(1, 8):
            dots_col(it, k).wait_send()
        for k in range(1, 16):
            dots_row(it, k).wait_send()
        return carry

    lax.fori_loop(0, ITERS, drain, 0)


def body(right_side, diag_term, near_pairs, near_tiles, far_pairs, far_factors):
    k_near, k_far = near_tiles.shape[0], far_factors.shape[0]
    field = jax.ShapeDtypeStruct((4, 32, 256), F32)
    vmem = pl.BlockSpec(memory_space=pltpu.VMEM)
    hbm = pl.BlockSpec(memory_space=pl.ANY)
    xa, ra = pl.pallas_call(
        kernel,
        out_shape=(field, field),
        in_specs=[vmem, vmem, vmem, vmem, hbm, hbm],
        out_specs=(vmem, vmem),
        scratch_shapes=[
            pltpu.VMEM((k_near, 256, 256), BF16),
            pltpu.VMEM((k_near, 256, 256), BF16),
            pltpu.VMEM((k_far, 2, 32, 256), BF16),
            pltpu.VMEM((k_near + 1, 32, 256), F32),
            pltpu.VMEM((k_far + 1, 32, 256), F32),
            pltpu.VMEM((k_near + 1, 32, 256), F32),
            pltpu.VMEM((k_far + 1, 32, 256), F32),
            pltpu.VMEM((ITERS, 32, 32, 256), BF16),
            pltpu.VMEM((ITERS, 32, 32, 256), BF16),
            pltpu.VMEM((64, 32, 256), BF16),
            pltpu.VMEM((64, 32, 256), F32),
            pltpu.VMEM((ITERS, 2, 4, 4, 32, 256), BF16),
            pltpu.VMEM((ITERS, 2, 4, 4, 32, 256), BF16),
            pltpu.VMEM((ITERS, 4, 4, 32, 256), BF16),
            pltpu.VMEM((ITERS, 4, 4, 32, 256), BF16),
            pltpu.VMEM((ITERS, 3, 4, 32, 256), BF16),
            pltpu.VMEM((ITERS, 3, 4, 32, 256), BF16),
            pltpu.VMEM((ITERS, 3, 4, 32, 256), BF16),
            pltpu.VMEM((ITERS, 4, 32, 256), BF16),
            pltpu.VMEM((ITERS, 4, 32, 256), BF16),
            pltpu.VMEM((ITERS, 4, 32, 256), BF16),
            pltpu.VMEM((ITERS, 3, 4, 32, 256), BF16),
            pltpu.VMEM((ITERS, 8, 1, 128), F32),
            pltpu.VMEM((ITERS, 16, 1, 128), F32),
            pltpu.VMEM((4, 32, 256), F32),
            pltpu.VMEM((4, 32, 256), F32),
            pltpu.VMEM((2, 32, 128), F32),
            pltpu.VMEM((2, 32, 128), F32),
            pltpu.VMEM((32, 256), F32),
            pltpu.VMEM((8, 128), jnp.int32),
            pltpu.VMEM((16, 128), jnp.int32),
            pltpu.SMEM((16, 128), jnp.int32),
            pltpu.SemaphoreType.DMA((ITERS, N_SEM)),
            pltpu.SemaphoreType.DMA((ITERS, N_SEM)),
            pltpu.SemaphoreType.DMA((3,)),
        ],
        compiler_params=pltpu.CompilerParams(
            collective_id=0, has_side_effects=True, vmem_limit_bytes=60 * 2**20
        ),
    )(right_side, diag_term, near_pairs, far_pairs, near_tiles, far_factors)

    def tail(a, b, c, d):
        c[...] = a[...]
        d[...] = b[...]

    return pl.pallas_call(tail, out_shape=(field, field), in_specs=[vmem, vmem], out_specs=(vmem, vmem))(xa, ra)


def solution(mesh):
    placed = (
        P(("row", "col"), None, None),
        P(("row", "col"), None),
        P(None, ("row", "col")),
        P(("row", "col"), None, None),
        P(None, ("row", "col")),
        P(("row", "col"), None, None, None),
    )
    return jax.shard_map(
        body,
        mesh=mesh,
        in_specs=placed,
        out_specs=(P(("row", "col"), None, None), P(("row", "col"), None, None)),
        check_vma=False,
    )
```

```python
import functools

import jax
import jax.numpy as jnp
from jax import lax
from jax.experimental import pallas as pl
from jax.experimental.pallas import tpu as pltpu
from jax.sharding import PartitionSpec as P

ITERS = 3
MESH = pl.DeviceIdType.MESH
NEAR_UNROLL = 32
FAR_UNROLL = 12
F32 = jnp.float32
BF16 = jnp.bfloat16

XO_Z = 0
XO_SIB = 3
XN_ROW = 7
XN_SIB = 11
PR_NEXT = 15
PR_OWN = 16
RNZ = 17
RN = 20
RF = 46
RO = 21
AR_COL = 24
AR_ROW = 31
N_SEM = 47


def sorted_tables(key, source, dummy):
    sub = lax.broadcasted_iota(jnp.int32, (128, 128), 0)
    lane = lax.broadcasted_iota(jnp.int32, (128, 128), 1)
    eye = sub == lane
    packed = key + 128 * source + 16384 * lane[:1]
    column = jnp.sum(jnp.where(eye, packed, 0), axis=1, keepdims=True)
    key_col = column & 127
    before = (key < key_col) | ((key == key_col) & (lane < sub))
    rank = jnp.sum(before.astype(jnp.int32), axis=1, keepdims=True)
    ordered = jnp.sum(jnp.where(rank == lane, column, 0), axis=0, keepdims=True)
    upto = jnp.sum((key_col <= lane).astype(jnp.int32), axis=0, keepdims=True)
    equal = jnp.sum((key_col == lane).astype(jnp.int32), axis=0, keepdims=True)
    last = jnp.where(equal > 0, upto - 1, dummy)
    return [ordered >> 14, (ordered >> 7) & 127, ordered & 127, last]


def kernel(
    b_ref, diag_ref, near_pairs, far_pairs, tiles_hbm, fac_hbm, x_ref, r_ref,
    tiles, turned, fac, pn, pf, pn2, pf2, xo, xn, ext, acc1, stn, sto, prn, pro, zsn, zso, rnz, xs, rn, rf, ro, ar1, ar2,
    p_ref, q_ref, gd, sc, dots, pairs, tabv, tab, ss, rs, ls,
):
    g = lax.axis_index("row")
    me = lax.axis_index("col")
    n_row = lax.axis_size("row")
    n_col = lax.axis_size("col")
    z, core = me // 2, lax.rem(me, 2)
    n_z = n_col // 2
    sib = z * 2 + (1 - core)
    nxt, prv = lax.rem(g + 1, n_row), lax.rem(g + n_row - 1, n_row)
    at_z = [lax.rem(z + d, n_z) for d in range(n_z)]
    at_col = [lax.rem(me + k, n_col) for k in range(n_col)]
    at_row = [lax.rem(g + k, n_row) for k in range(n_row)]
    k_near = tiles.shape[0]
    k_far = fac.shape[0]

    def zc(d):
        return at_z[d % n_z] * 2 + core

    def zs(d):
        return at_z[d % n_z] * 2 + (1 - core)

    def rdma(it, idx, src, dst, row, col):
        return pltpu.make_async_remote_copy(
            src_ref=src, dst_ref=dst, send_sem=ss.at[it, idx], recv_sem=rs.at[it, idx],
            device_id=(row, col), device_id_type=MESH,
        )

    def shard(ref, it, col):
        return ref.at[it, pl.ds(col * 4, 4)]

    load_tiles = pltpu.make_async_copy(tiles_hbm, tiles, ls.at[0])
    load_fac = pltpu.make_async_copy(fac_hbm, fac, ls.at[1])
    load_tiles.start()
    load_fac.start()

    barrier = pltpu.get_barrier_semaphore()
    peers = [(g, at_col[k]) for k in range(1, n_col)]
    peers += [(at_row[k], me) for k in range(1, n_row)]
    peers += [(nxt, sib), (prv, sib)]
    for peer in peers:
        pl.semaphore_signal(barrier, inc=1, device_id=peer, device_id_type=MESH)

    sub = lax.broadcasted_iota(jnp.int32, (32, 128), 0)
    lane = lax.broadcasted_iota(jnp.int32, (32, 128), 1)

    def lane_sum(field):
        return jnp.sum(field[:, :128] + field[:, 128:], axis=1, keepdims=True)

    def to_row(cols):
        total = jnp.zeros((32, 128), F32)
        for j, col in enumerate(cols):
            total += jnp.where(lane == sub + 32 * j, col, 0.0)
        return jnp.sum(total, axis=0, keepdims=True)

    def to_col(row, j):
        return jnp.sum(jnp.where(lane == sub + 32 * j, row, 0.0), axis=1, keepdims=True)

    def wide(col):
        return jnp.broadcast_to(col, (32, 128))

    total = jnp.zeros((32, 256), F32)
    for j in range(4):
        r = b_ref[j]
        r_ref[j] = r
        x_ref[j] = jnp.zeros((32, 256), F32)
        p_ref[j] = jnp.zeros((32, 256), F32)
        q_ref[j] = jnp.zeros((32, 256), F32)
        xo[0, me * 4 + j] = r.astype(BF16)
        total += r * r
    gd[0] = wide(lane_sum(total))
    gd[1] = jnp.zeros((32, 128), F32)
    sc[0] = jnp.ones((32, 128), F32)
    sc[1] = jnp.zeros((32, 128), F32)
    for ref in (pn, pn2):
        ref[k_near] = jnp.zeros((32, 256), F32)
    for ref in (pf, pf2):
        ref[k_far] = jnp.zeros((32, 256), F32)

    pairs[...] = jnp.zeros((8, 128), jnp.int32)
    pairs[pl.ds(0, 3), pl.ds(0, k_near)] = near_pairs[...]
    pairs[pl.ds(3, 3), pl.ds(0, k_far)] = far_pairs[...]
    tables = []
    for first, count in ((0, k_near), (3, k_far)):
        row_id = jnp.clip(pairs[pl.ds(first, 1), :] - g * 32, 0, 31)
        col_id = jnp.clip(pairs[pl.ds(first + 1, 1), :] - g * 32, 0, 63)
        live = pairs[pl.ds(first + 2, 1), :] != 0
        tables += sorted_tables(jnp.where(live, col_id, 64), row_id, count)
        tables += sorted_tables(jnp.where(live, row_id, 64), col_id, count)
    for i, line in enumerate(tables):
        tabv[pl.ds(i, 1), :] = line
    copy_tab = pltpu.make_async_copy(tabv, tab, ls.at[2])
    copy_tab.start()

    pl.semaphore_wait(barrier, len(peers))

    def first_sends(it):
        mine = shard(xo, it, me)
        return [
            rdma(it, XO_Z + d - 1, mine, mine, g, zc(d)) for d in (2, 1, 3)
        ] + [
            rdma(it, XO_SIB, mine, mine, g, sib),
            rdma(it, XN_ROW, mine, shard(xn, it, me), prv, me),
        ]

    def from_z(it, d):
        here = shard(xo, it, zc(-d))
        return rdma(it, XO_Z + d - 1, here, here, g, zc(d))

    def relays(it, d):
        here = shard(xo, it, zc(-d))
        copies = [rdma(it, XO_SIB + d, here, here, g, sib)]
        if d == 2:
            there = shard(xn, it, zc(-d))
            copies.append(rdma(it, XN_ROW + d, here, there, prv, me))
            copies.append(rdma(it, XN_SIB + d, here, there, prv, sib))
        return copies

    def next_to_z(it, d):
        here = shard(xn, it, me)
        return rdma(it, XN_ROW + d, here, here, g, zc(d))

    def from_sib(it, d):
        here = shard(xo, it, zs(-d))
        return rdma(it, XO_SIB + d, here, here, g, sib)

    def next_from_row(it, d):
        here = shard(xn, it, zc(-d))
        return rdma(it, XN_ROW + d, here, here, prv, me)

    def next_to_sib(it, d):
        here = shard(xn, it, zc(-d))
        return rdma(it, XN_SIB + d, here, here, g, sib)

    def next_from_sib(it, d):
        here = shard(xn, it, zs(-d))
        return rdma(it, XN_SIB + d, here, here, g, sib)

    def pair_next(it):
        return rdma(it, PR_NEXT, stn.at[it, 1 - core], prn.at[it], g, sib)

    def pair_own(it):
        return rdma(it, PR_OWN, sto.at[it, 1 - core], pro.at[it], g, sib)

    def terms_next(it, d):
        return rdma(it, RNZ + d - 1, zsn.at[it, d - 1], rnz.at[it, d - 1], g, zc(d))

    def terms_far(it):
        return rdma(it, RF, zsn.at[it, 1], rf.at[it], nxt, me)

    def terms_over(it):
        return rdma(it, RN, xs.at[it], rn.at[it], nxt, me)

    def terms_own(it, d):
        return rdma(it, RO + d - 1, zso.at[it, d - 1], ro.at[it, d - 1], g, zc(d))

    def dots_col(it, k):
        return rdma(it, AR_COL + k - 1, ar1.at[it, me], ar1.at[it, me], g, at_col[k])

    def dots_col_in(it, k):
        here = ar1.at[it, at_col[n_col - k]]
        return rdma(it, AR_COL + k - 1, here, here, g, at_col[k])

    def dots_row(it, k):
        return rdma(it, AR_ROW + k - 1, ar2.at[it, g], ar2.at[it, g], at_row[k], me)

    def dots_row_in(it, k):
        here = ar2.at[it, at_row[n_row - k]]
        return rdma(it, AR_ROW + k - 1, here, here, at_row[k], me)

    def near_phase(base, blocks, sums, first, last, acc, beside=None):
        unroll = min(NEAR_UNROLL, last - first)

        def step(block, acc):
            for u in range(unroll):
                if beside is not None:
                    beside(u)
                k = first + block * unroll + u
                field = ext[tab[base + 1, k]]
                tile = blocks[tab[base, k]]
                keep = (tab[base + 2, k] == tab[base + 2, lax.max(k - 1, 0)]).astype(F32)
                term = lax.dot_general(field, tile, (((1,), (0,)), ((), ())), preferred_element_type=F32)
                acc = acc * keep + term
                sums[k] = acc
            return acc

        return lax.fori_loop(0, (last - first) // unroll, step, acc)

    def far_phase(base, first, second, sums):
        lanes = lax.broadcasted_iota(jnp.int32, (256, 256), 1) // 32
        rows = lax.broadcasted_iota(jnp.int32, (256, 256), 0) // 32
        mask = lanes == rows

        def step(block, acc):
            for u in range(FAR_UNROLL):
                start = (block * FAR_UNROLL + u) * 8
                fields, lefts, rights = [], [], []
                for q in range(8):
                    slot = tab[base, start + q]
                    fields.append(ext[tab[base + 1, start + q]])
                    lefts.append(fac[slot, first])
                    rights.append(fac[slot, second])
                field = jnp.concatenate(fields, axis=0)
                left = jnp.concatenate(lefts, axis=0)
                right = jnp.concatenate(rights, axis=0)
                inner = lax.dot_general(field, left, (((1,), (1,)), ((), ())), preferred_element_type=F32)
                inner = jnp.where(mask, inner, 0.0).astype(BF16)
                term = lax.dot_general(inner, right, (((1,), (0,)), ((), ())), preferred_element_type=F32)
                for q in range(8):
                    k = start + q
                    keep = (tab[base + 2, k] == tab[base + 2, lax.max(k - 1, 0)]).astype(F32)
                    acc = acc * keep + term[q * 32 : q * 32 + 32]
                    sums[k] = acc
            return acc

        lax.fori_loop(0, k_far // (8 * FAR_UNROLL), step, jnp.zeros((32, 256), F32))

    for copy in first_sends(0):
        copy.start()
    copy_tab.wait()
    load_tiles.wait()

    def turn(block, carry):
        for u in range(4):
            turned[block * 4 + u] = tiles[block * 4 + u].T
        return carry

    lax.fori_loop(0, k_near // 4, turn, 0)
    load_fac.wait()

    def iteration(it, carry):
        for d in (1, 3):
            from_z(it, d).wait_recv()
            for copy in relays(it, d):
                copy.start()
        next_from_row(it, 0).wait_recv()
        for d in (1, 3):
            next_to_z(it, d).start()
        from_z(it, 2).wait_recv()
        for copy in relays(it, 2):
            copy.start()
        next_to_sib(it, 0).start()
        for d in (0, 1, 3, 2):
            from_sib(it, d).wait_recv()
        ext[pl.ds(0, 32)] = xo[it]

        zero = jnp.zeros((32, 256), F32)
        far_phase(8, 0, 1, pf)
        acc = near_phase(0, tiles, pn, 0, k_near // 2, zero)
        near_phase(0, tiles, pn, k_near // 2, k_near, acc)
        for d in (1, 3):
            next_from_row(it, d).wait_recv()
            next_to_sib(it, d).start()

        def fold_next(chunk, j, c):
            place = chunk * 8 + c * 4 + j + 32
            out = pn[tab[3, place]] + pf[tab[11, place]]
            acc1[place] = out
            stn[it, c, chunk, j] = out.astype(BF16)

        for chunk in range(4):
            for j in range(4):
                fold_next(chunk, j, 1 - core)
        pair_next(it).start()

        next_from_row(it, 2).wait_recv()
        for d in (0, 1, 3, 2):
            next_from_sib(it, d).wait_recv()
        ext[pl.ds(32, 32)] = xn[it]

        dots[...] = zero

        def fold_own(i):
            out = pn[tab[3, i]] + pf[tab[11, i]]
            acc1[i] = out
            dots[...] += out * ext[i].astype(F32) + acc1[i + 32] * ext[i + 32].astype(F32)

        acc = near_phase(4, turned, pn2, 0, 16, zero, lambda i: fold_next(i // 4, i % 4, core))

        pair_next(it).wait_recv()
        for d in (2, 1, 3):
            chunk = at_z[d]
            for j in range(4):
                zsn[it, d - 1, j] = (
                    stn[it, core, chunk, j].astype(F32) + prn[it, chunk, j].astype(F32)
                ).astype(BF16)
            (terms_far(it) if d == 2 else terms_next(it, d)).start()

        acc = near_phase(4, turned, pn2, 16, 48, acc, fold_own)
        total = dots[...] * 2.0
        for j in range(4):
            r = r_ref[j]
            total += (diag_ref[pl.ds(j, 1), :] * r) * r
        ar1[it, me] = to_row([lane_sum(total), gd[0], gd[1]])
        for k in range(1, 8):
            dots_col(it, k).start()

        far_phase(12, 1, 0, pf2)
        near_phase(4, turned, pn2, 48, k_near, acc)

        def fold_rows(chunk, c):
            for j in range(4):
                place = chunk * 8 + c * 4 + j
                out = acc1[place] + (pn2[tab[7, place]] + pf2[tab[15, place]])
                sto[it, c, chunk, j] = out.astype(BF16)
            return c

        lax.fori_loop(0, 4, fold_rows, 1 - core)
        pair_own(it).start()
        lax.fori_loop(0, 4, fold_rows, core)
        row = jnp.zeros((1, 128), F32)
        for k in range(1, 8):
            dots_col_in(it, k).wait_recv()
        for k in range(8):
            row += ar1[it, k]
        ar2[it, g] = row
        for k in range(1, 16):
            dots_row(it, k).start()
        pair_own(it).wait_recv()
        for d in (1, 3, 2):
            chunk = at_z[d]
            if d == 2:
                terms_far(it).wait_recv()
            for j in range(4):
                out = sto[it, core, chunk, j].astype(F32) + pro[it, chunk, j].astype(F32)
                if d == 2:
                    out += rf[it, j].astype(F32)
                zso[it, d - 1, j] = out.astype(BF16)
            terms_own(it, d).start()

        for d in (1, 3):
            terms_next(it, d).wait_recv()
        for j in range(4):
            out = stn[it, core, z, j].astype(F32) + prn[it, z, j].astype(F32)
            for d in (0, 2):
                out += rnz[it, d, j].astype(F32)
            xs[it, j] = out.astype(BF16)
        terms_over(it).start()

        row = jnp.zeros((1, 128), F32)
        for k in range(1, 16):
            dots_row_in(it, k).wait_recv()
        for k in range(16):
            row += ar2[it, k]
        delta, gamma, eta = to_col(row, 0), to_col(row, 1), to_col(row, 2)
        beta = gamma / sc[0][:, :1]
        curvature = delta + 2.0 * beta * eta + beta * beta * sc[1][:, :1]
        alpha = gamma / curvature
        sc[0] = wide(gamma)
        sc[1] = wide(curvature)

        for j in range(4):
            r = r_ref[j]
            p = r + beta * p_ref[j]
            p_ref[j] = p
            x_ref[j] = x_ref[j] + alpha * p
            q = diag_ref[pl.ds(j, 1), :] * r + beta * q_ref[j]
            q_ref[j] = q + (sto[it, core, z, j].astype(F32) + pro[it, z, j].astype(F32))
        for d in (1, 3, 2):
            terms_own(it, d).wait_recv()
        terms_over(it).wait_recv()
        total = jnp.zeros((32, 256), F32)
        cross = jnp.zeros((32, 256), F32)
        for j in range(4):
            q = q_ref[j] + rn[it, j].astype(F32)
            for d in range(3):
                q += ro[it, d, j].astype(F32)
            q_ref[j] = q
            r = r_ref[j] - alpha * q
            r_ref[j] = r

            @pl.when(it < ITERS - 1)
            def _():
                xo[lax.min(it + 1, ITERS - 1), me * 4 + j] = r.astype(BF16)

            total += r * r
            cross += r * q

        @pl.when(it < ITERS - 1)
        def _():
            for copy in first_sends(it + 1):
                copy.start()

        gd[0] = wide(lane_sum(total))
        gd[1] = wide(lane_sum(cross))
        return carry

    lax.fori_loop(0, ITERS, iteration, 0)

    def drain(it, carry):
        for copy in first_sends(it):
            copy.wait_send()
        for d in (1, 2, 3):
            for copy in relays(it, d):
                copy.wait_send()
            terms_own(it, d).wait_send()
        for d in (1, 3):
            next_to_z(it, d).wait_send()
            terms_next(it, d).wait_send()
        terms_far(it).wait_send()
        terms_over(it).wait_send()
        for d in (0, 1, 3):
            next_to_sib(it, d).wait_send()
        pair_next(it).wait_send()
        pair_own(it).wait_send()
        for k in range(1, 8):
            dots_col(it, k).wait_send()
        for k in range(1, 16):
            dots_row(it, k).wait_send()
        return carry

    lax.fori_loop(0, ITERS, drain, 0)


def body(right_side, diag_term, near_pairs, near_tiles, far_pairs, far_factors):
    k_near, k_far = near_tiles.shape[0], far_factors.shape[0]
    field = jax.ShapeDtypeStruct((4, 32, 256), F32)
    vmem = pl.BlockSpec(memory_space=pltpu.VMEM)
    hbm = pl.BlockSpec(memory_space=pl.ANY)
    xa, ra = pl.pallas_call(
        kernel,
        out_shape=(field, field),
        in_specs=[vmem, vmem, vmem, vmem, hbm, hbm],
        out_specs=(vmem, vmem),
        scratch_shapes=[
            pltpu.VMEM((k_near, 256, 256), BF16),
            pltpu.VMEM((k_near, 256, 256), BF16),
            pltpu.VMEM((k_far, 2, 32, 256), BF16),
            pltpu.VMEM((k_near + 1, 32, 256), F32),
            pltpu.VMEM((k_far + 1, 32, 256), F32),
            pltpu.VMEM((k_near + 1, 32, 256), F32),
            pltpu.VMEM((k_far + 1, 32, 256), F32),
            pltpu.VMEM((ITERS, 32, 32, 256), BF16),
            pltpu.VMEM((ITERS, 32, 32, 256), BF16),
            pltpu.VMEM((64, 32, 256), BF16),
            pltpu.VMEM((64, 32, 256), F32),
            pltpu.VMEM((ITERS, 2, 4, 4, 32, 256), BF16),
            pltpu.VMEM((ITERS, 2, 4, 4, 32, 256), BF16),
            pltpu.VMEM((ITERS, 4, 4, 32, 256), BF16),
            pltpu.VMEM((ITERS, 4, 4, 32, 256), BF16),
            pltpu.VMEM((ITERS, 3, 4, 32, 256), BF16),
            pltpu.VMEM((ITERS, 3, 4, 32, 256), BF16),
            pltpu.VMEM((ITERS, 3, 4, 32, 256), BF16),
            pltpu.VMEM((ITERS, 4, 32, 256), BF16),
            pltpu.VMEM((ITERS, 4, 32, 256), BF16),
            pltpu.VMEM((ITERS, 4, 32, 256), BF16),
            pltpu.VMEM((ITERS, 3, 4, 32, 256), BF16),
            pltpu.VMEM((ITERS, 8, 1, 128), F32),
            pltpu.VMEM((ITERS, 16, 1, 128), F32),
            pltpu.VMEM((4, 32, 256), F32),
            pltpu.VMEM((4, 32, 256), F32),
            pltpu.VMEM((2, 32, 128), F32),
            pltpu.VMEM((2, 32, 128), F32),
            pltpu.VMEM((32, 256), F32),
            pltpu.VMEM((8, 128), jnp.int32),
            pltpu.VMEM((16, 128), jnp.int32),
            pltpu.SMEM((16, 128), jnp.int32),
            pltpu.SemaphoreType.DMA((ITERS, N_SEM)),
            pltpu.SemaphoreType.DMA((ITERS, N_SEM)),
            pltpu.SemaphoreType.DMA((3,)),
        ],
        compiler_params=pltpu.CompilerParams(
            collective_id=0, has_side_effects=True, vmem_limit_bytes=60 * 2**20
        ),
    )(right_side, diag_term, near_pairs, far_pairs, near_tiles, far_factors)

    def tail(a, b, c, d):
        c[...] = a[...]
        d[...] = b[...]

    return pl.pallas_call(tail, out_shape=(field, field), in_specs=[vmem, vmem], out_specs=(vmem, vmem))(xa, ra)


def solution(mesh):
    placed = (
        P(("row", "col"), None, None),
        P(("row", "col"), None),
        P(None, ("row", "col")),
        P(("row", "col"), None, None),
        P(None, ("row", "col")),
        P(("row", "col"), None, None, None),
    )
    return jax.shard_map(
        body,
        mesh=mesh,
        in_specs=placed,
        out_specs=(P(("row", "col"), None, None), P(("row", "col"), None, None)),
        check_vma=False,
    )
```

```python
import functools

import jax
import jax.numpy as jnp
from jax import lax
from jax.experimental import pallas as pl
from jax.experimental.pallas import tpu as pltpu
from jax.sharding import PartitionSpec as P

ITERS = 3
MESH = pl.DeviceIdType.MESH
NEAR_UNROLL = 32
FAR_UNROLL = 12
F32 = jnp.float32
BF16 = jnp.bfloat16

XO_Z = 0
XO_SIB = 3
XN_ROW = 7
XN_SIB = 11
PR_NEXT = 15
PR_OWN = 16
RNZ = 17
RN = 20
RF = 46
RO = 21
AR_COL = 24
AR_ROW = 31
N_SEM = 47


def sorted_tables(key, source, dummy):
    sub = lax.broadcasted_iota(jnp.int32, (128, 128), 0)
    lane = lax.broadcasted_iota(jnp.int32, (128, 128), 1)
    eye = sub == lane
    packed = key + 128 * source + 16384 * lane[:1]
    column = jnp.sum(jnp.where(eye, packed, 0), axis=1, keepdims=True)
    key_col = column & 127
    before = (key < key_col) | ((key == key_col) & (lane < sub))
    rank = jnp.sum(before.astype(jnp.int32), axis=1, keepdims=True)
    ordered = jnp.sum(jnp.where(rank == lane, column, 0), axis=0, keepdims=True)
    upto = jnp.sum((key_col <= lane).astype(jnp.int32), axis=0, keepdims=True)
    equal = jnp.sum((key_col == lane).astype(jnp.int32), axis=0, keepdims=True)
    last = jnp.where(equal > 0, upto - 1, dummy)
    return [ordered >> 14, (ordered >> 7) & 127, ordered & 127, last]


def kernel(
    b_ref, diag_ref, near_pairs, far_pairs, tiles_hbm, fac_hbm, x_ref, r_ref,
    tiles, turned, fac, pn, pf, pn2, pf2, xo, xn, ext, acc1, stn, sto, prn, pro, zsn, zso, rnz, xs, rn, rf, ro, ar1, ar2,
    p_ref, q_ref, gd, sc, dots, pairs, tabv, tab, ss, rs, ls,
):
    g = lax.axis_index("row")
    me = lax.axis_index("col")
    n_row = lax.axis_size("row")
    n_col = lax.axis_size("col")
    z, core = me // 2, lax.rem(me, 2)
    n_z = n_col // 2
    sib = z * 2 + (1 - core)
    nxt, prv = lax.rem(g + 1, n_row), lax.rem(g + n_row - 1, n_row)
    at_z = [lax.rem(z + d, n_z) for d in range(n_z)]
    at_col = [lax.rem(me + k, n_col) for k in range(n_col)]
    at_row = [lax.rem(g + k, n_row) for k in range(n_row)]
    k_near = tiles.shape[0]
    k_far = fac.shape[0]

    def zc(d):
        return at_z[d % n_z] * 2 + core

    def zs(d):
        return at_z[d % n_z] * 2 + (1 - core)

    def rdma(it, idx, src, dst, row, col):
        return pltpu.make_async_remote_copy(
            src_ref=src, dst_ref=dst, send_sem=ss.at[it, idx], recv_sem=rs.at[it, idx],
            device_id=(row, col), device_id_type=MESH,
        )

    def shard(ref, it, col):
        return ref.at[it, pl.ds(col * 4, 4)]

    load_tiles = pltpu.make_async_copy(tiles_hbm, tiles, ls.at[0])
    load_fac = pltpu.make_async_copy(fac_hbm, fac, ls.at[1])
    load_tiles.start()
    load_fac.start()

    barrier = pltpu.get_barrier_semaphore()
    peers = [(g, at_col[k]) for k in range(1, n_col)]
    peers += [(at_row[k], me) for k in range(1, n_row)]
    peers += [(nxt, sib), (prv, sib)]
    for peer in peers:
        pl.semaphore_signal(barrier, inc=1, device_id=peer, device_id_type=MESH)

    sub = lax.broadcasted_iota(jnp.int32, (32, 128), 0)
    lane = lax.broadcasted_iota(jnp.int32, (32, 128), 1)

    def lane_sum(field):
        return jnp.sum(field[:, :128] + field[:, 128:], axis=1, keepdims=True)

    def to_row(cols):
        total = jnp.zeros((32, 128), F32)
        for j, col in enumerate(cols):
            total += jnp.where(lane == sub + 32 * j, col, 0.0)
        return jnp.sum(total, axis=0, keepdims=True)

    def to_col(row, j):
        return jnp.sum(jnp.where(lane == sub + 32 * j, row, 0.0), axis=1, keepdims=True)

    def wide(col):
        return jnp.broadcast_to(col, (32, 128))

    total = jnp.zeros((32, 256), F32)
    for j in range(4):
        r = b_ref[j]
        r_ref[j] = r
        x_ref[j] = jnp.zeros((32, 256), F32)
        p_ref[j] = jnp.zeros((32, 256), F32)
        q_ref[j] = jnp.zeros((32, 256), F32)
        xo[0, me * 4 + j] = r.astype(BF16)
        total += r * r
    gd[0] = wide(lane_sum(total))
    gd[1] = jnp.zeros((32, 128), F32)
    sc[0] = jnp.ones((32, 128), F32)
    sc[1] = jnp.zeros((32, 128), F32)
    for ref in (pn, pn2):
        ref[k_near] = jnp.zeros((32, 256), F32)
    for ref in (pf, pf2):
        ref[k_far] = jnp.zeros((32, 256), F32)

    pairs[...] = jnp.zeros((8, 128), jnp.int32)
    pairs[pl.ds(0, 3), pl.ds(0, k_near)] = near_pairs[...]
    pairs[pl.ds(3, 3), pl.ds(0, k_far)] = far_pairs[...]
    tables = []
    for first, count in ((0, k_near), (3, k_far)):
        row_id = jnp.clip(pairs[pl.ds(first, 1), :] - g * 32, 0, 31)
        col_id = jnp.clip(pairs[pl.ds(first + 1, 1), :] - g * 32, 0, 63)
        live = pairs[pl.ds(first + 2, 1), :] != 0
        tables += sorted_tables(jnp.where(live, col_id, 64), row_id, count)
        tables += sorted_tables(jnp.where(live, row_id, 64), col_id, count)
    for i, line in enumerate(tables):
        tabv[pl.ds(i, 1), :] = line
    copy_tab = pltpu.make_async_copy(tabv, tab, ls.at[2])
    copy_tab.start()

    pl.semaphore_wait(barrier, len(peers))

    def first_sends(it):
        mine = shard(xo, it, me)
        return [
            rdma(it, XO_Z + d - 1, mine, mine, g, zc(d)) for d in (2, 1, 3)
        ] + [
            rdma(it, XO_SIB, mine, mine, g, sib),
            rdma(it, XN_ROW, mine, shard(xn, it, me), prv, me),
            rdma(it, XN_SIB, mine, shard(xn, it, me), prv, sib),
        ]

    def from_z(it, d):
        here = shard(xo, it, zc(-d))
        return rdma(it, XO_Z + d - 1, here, here, g, zc(d))

    def relays(it, d):
        here = shard(xo, it, zc(-d))
        copies = [rdma(it, XO_SIB + d, here, here, g, sib)]
        if d == 2:
            there = shard(xn, it, zc(-d))
            copies.append(rdma(it, XN_ROW + d, here, there, prv, me))
            copies.append(rdma(it, XN_SIB + d, here, there, prv, sib))
        return copies

    def next_to_z(it, d):
        here = shard(xn, it, me)
        return rdma(it, XN_ROW + d, here, here, g, zc(d))

    def from_sib(it, d):
        here = shard(xo, it, zs(-d))
        return rdma(it, XO_SIB + d, here, here, g, sib)

    def next_from_row(it, d):
        here = shard(xn, it, zc(-d))
        return rdma(it, XN_ROW + d, here, here, prv, me)

    def next_to_sib(it, d):
        here = shard(xn, it, zc(-d))
        return rdma(it, XN_SIB + d, here, here, g, sib)

    def next_from_sib(it, d):
        here = shard(xn, it, zs(-d))
        return rdma(it, XN_SIB + d, here, here, g, sib)

    def pair_next(it):
        return rdma(it, PR_NEXT, stn.at[it, 1 - core], prn.at[it], g, sib)

    def pair_own(it):
        return rdma(it, PR_OWN, sto.at[it, 1 - core], pro.at[it], g, sib)

    def terms_next(it, d):
        return rdma(it, RNZ + d - 1, zsn.at[it, d - 1], rnz.at[it, d - 1], g, zc(d))

    def terms_far(it):
        return rdma(it, RF, zsn.at[it, 1], rf.at[it], nxt, me)

    def terms_over(it):
        return rdma(it, RN, xs.at[it], rn.at[it], nxt, me)

    def terms_own(it, d):
        return rdma(it, RO + d - 1, zso.at[it, d - 1], ro.at[it, d - 1], g, zc(d))

    def dots_col(it, k):
        return rdma(it, AR_COL + k - 1, ar1.at[it, me], ar1.at[it, me], g, at_col[k])

    def dots_col_in(it, k):
        here = ar1.at[it, at_col[n_col - k]]
        return rdma(it, AR_COL + k - 1, here, here, g, at_col[k])

    def dots_row(it, k):
        return rdma(it, AR_ROW + k - 1, ar2.at[it, g], ar2.at[it, g], at_row[k], me)

    def dots_row_in(it, k):
        here = ar2.at[it, at_row[n_row - k]]
        return rdma(it, AR_ROW + k - 1, here, here, at_row[k], me)

    def near_phase(base, blocks, sums, first, last, acc, beside=None):
        unroll = min(NEAR_UNROLL, last - first)

        def step(block, acc):
            for u in range(unroll):
                if beside is not None:
                    beside(u)
                k = first + block * unroll + u
                field = ext[tab[base + 1, k]]
                tile = blocks[tab[base, k]]
                keep = (tab[base + 2, k] == tab[base + 2, lax.max(k - 1, 0)]).astype(F32)
                term = lax.dot_general(field, tile, (((1,), (0,)), ((), ())), preferred_element_type=F32)
                acc = acc * keep + term
                sums[k] = acc
            return acc

        return lax.fori_loop(0, (last - first) // unroll, step, acc)

    def far_phase(base, first, second, sums):
        lanes = lax.broadcasted_iota(jnp.int32, (256, 256), 1) // 32
        rows = lax.broadcasted_iota(jnp.int32, (256, 256), 0) // 32
        mask = lanes == rows

        def step(block, acc):
            for u in range(FAR_UNROLL):
                start = (block * FAR_UNROLL + u) * 8
                fields, lefts, rights = [], [], []
                for q in range(8):
                    slot = tab[base, start + q]
                    fields.append(ext[tab[base + 1, start + q]])
                    lefts.append(fac[slot, first])
                    rights.append(fac[slot, second])
                field = jnp.concatenate(fields, axis=0)
                left = jnp.concatenate(lefts, axis=0)
                right = jnp.concatenate(rights, axis=0)
                inner = lax.dot_general(field, left, (((1,), (1,)), ((), ())), preferred_element_type=F32)
                inner = jnp.where(mask, inner, 0.0).astype(BF16)
                term = lax.dot_general(inner, right, (((1,), (0,)), ((), ())), preferred_element_type=F32)
                for q in range(8):
                    k = start + q
                    keep = (tab[base + 2, k] == tab[base + 2, lax.max(k - 1, 0)]).astype(F32)
                    acc = acc * keep + term[q * 32 : q * 32 + 32]
                    sums[k] = acc
            return acc

        lax.fori_loop(0, k_far // (8 * FAR_UNROLL), step, jnp.zeros((32, 256), F32))

    for copy in first_sends(0):
        copy.start()
    copy_tab.wait()
    load_tiles.wait()

    def turn(block, carry):
        for u in range(4):
            turned[block * 4 + u] = tiles[block * 4 + u].T
        return carry

    lax.fori_loop(0, k_near // 4, turn, 0)
    load_fac.wait()

    def iteration(it, carry):
        for d in (1, 3):
            from_z(it, d).wait_recv()
            for copy in relays(it, d):
                copy.start()
        next_from_row(it, 0).wait_recv()
        for d in (1, 3):
            next_to_z(it, d).start()
        from_z(it, 2).wait_recv()
        for copy in relays(it, 2):
            copy.start()
        for d in (0, 1, 3, 2):
            from_sib(it, d).wait_recv()
        ext[pl.ds(0, 32)] = xo[it]

        zero = jnp.zeros((32, 256), F32)
        far_phase(8, 0, 1, pf)
        acc = near_phase(0, tiles, pn, 0, k_near // 2, zero)
        near_phase(0, tiles, pn, k_near // 2, k_near, acc)
        for d in (1, 3):
            next_from_row(it, d).wait_recv()
            next_to_sib(it, d).start()

        def fold_next(chunk, j, c):
            place = chunk * 8 + c * 4 + j + 32
            out = pn[tab[3, place]] + pf[tab[11, place]]
            acc1[place] = out
            stn[it, c, chunk, j] = out.astype(BF16)

        for chunk in range(4):
            for j in range(4):
                fold_next(chunk, j, 1 - core)
        pair_next(it).start()

        next_from_row(it, 2).wait_recv()
        for d in (0, 1, 3, 2):
            next_from_sib(it, d).wait_recv()
        ext[pl.ds(32, 32)] = xn[it]

        dots[...] = zero

        def fold_own(i):
            out = pn[tab[3, i]] + pf[tab[11, i]]
            acc1[i] = out
            dots[...] += out * ext[i].astype(F32) + acc1[i + 32] * ext[i + 32].astype(F32)

        acc = near_phase(4, turned, pn2, 0, 16, zero, lambda i: fold_next(i // 4, i % 4, core))

        pair_next(it).wait_recv()
        for d in (2, 1, 3):
            chunk = at_z[d]
            for j in range(4):
                zsn[it, d - 1, j] = (
                    stn[it, core, chunk, j].astype(F32) + prn[it, chunk, j].astype(F32)
                ).astype(BF16)
            (terms_far(it) if d == 2 else terms_next(it, d)).start()

        acc = near_phase(4, turned, pn2, 16, 48, acc, fold_own)
        total = dots[...] * 2.0
        for j in range(4):
            r = r_ref[j]
            total += (diag_ref[pl.ds(j, 1), :] * r) * r
        ar1[it, me] = to_row([lane_sum(total), gd[0], gd[1]])
        for k in range(1, 8):
            dots_col(it, k).start()

        near_phase(4, turned, pn2, 48, k_near, acc)
        far_phase(12, 1, 0, pf2)

        def fold_rows(chunk, c):
            for j in range(4):
                place = chunk * 8 + c * 4 + j
                out = acc1[place] + (pn2[tab[7, place]] + pf2[tab[15, place]])
                sto[it, c, chunk, j] = out.astype(BF16)
            return c

        lax.fori_loop(0, 4, fold_rows, 1 - core)
        pair_own(it).start()
        lax.fori_loop(0, 4, fold_rows, core)
        row = jnp.zeros((1, 128), F32)
        for k in range(1, 8):
            dots_col_in(it, k).wait_recv()
        for k in range(8):
            row += ar1[it, k]
        ar2[it, g] = row
        for k in range(1, 16):
            dots_row(it, k).start()
        pair_own(it).wait_recv()
        for d in (1, 3, 2):
            chunk = at_z[d]
            if d == 2:
                terms_far(it).wait_recv()
            for j in range(4):
                out = sto[it, core, chunk, j].astype(F32) + pro[it, chunk, j].astype(F32)
                if d == 2:
                    out += rf[it, j].astype(F32)
                zso[it, d - 1, j] = out.astype(BF16)
            terms_own(it, d).start()

        for d in (1, 3):
            terms_next(it, d).wait_recv()
        for j in range(4):
            out = stn[it, core, z, j].astype(F32) + prn[it, z, j].astype(F32)
            for d in (0, 2):
                out += rnz[it, d, j].astype(F32)
            xs[it, j] = out.astype(BF16)
        terms_over(it).start()

        row = jnp.zeros((1, 128), F32)
        for k in range(1, 16):
            dots_row_in(it, k).wait_recv()
        for k in range(16):
            row += ar2[it, k]
        delta, gamma, eta = to_col(row, 0), to_col(row, 1), to_col(row, 2)
        beta = gamma / sc[0][:, :1]
        curvature = delta + 2.0 * beta * eta + beta * beta * sc[1][:, :1]
        alpha = gamma / curvature
        sc[0] = wide(gamma)
        sc[1] = wide(curvature)

        for j in range(4):
            r = r_ref[j]
            p = r + beta * p_ref[j]
            p_ref[j] = p
            x_ref[j] = x_ref[j] + alpha * p
            q = diag_ref[pl.ds(j, 1), :] * r + beta * q_ref[j]
            q_ref[j] = q + (sto[it, core, z, j].astype(F32) + pro[it, z, j].astype(F32))
        for d in (1, 3, 2):
            terms_own(it, d).wait_recv()
        terms_over(it).wait_recv()
        total = jnp.zeros((32, 256), F32)
        cross = jnp.zeros((32, 256), F32)
        for j in range(4):
            q = q_ref[j] + rn[it, j].astype(F32)
            for d in range(3):
                q += ro[it, d, j].astype(F32)
            q_ref[j] = q
            r = r_ref[j] - alpha * q
            r_ref[j] = r

            @pl.when(it < ITERS - 1)
            def _():
                xo[lax.min(it + 1, ITERS - 1), me * 4 + j] = r.astype(BF16)

            total += r * r
            cross += r * q

        @pl.when(it < ITERS - 1)
        def _():
            for copy in first_sends(it + 1):
                copy.start()

        gd[0] = wide(lane_sum(total))
        gd[1] = wide(lane_sum(cross))
        return carry

    lax.fori_loop(0, ITERS, iteration, 0)

    def drain(it, carry):
        for copy in first_sends(it):
            copy.wait_send()
        for d in (1, 2, 3):
            for copy in relays(it, d):
                copy.wait_send()
            terms_own(it, d).wait_send()
        for d in (1, 3):
            next_to_z(it, d).wait_send()
            terms_next(it, d).wait_send()
        terms_far(it).wait_send()
        terms_over(it).wait_send()
        for d in (1, 3):
            next_to_sib(it, d).wait_send()
        pair_next(it).wait_send()
        pair_own(it).wait_send()
        for k in range(1, 8):
            dots_col(it, k).wait_send()
        for k in range(1, 16):
            dots_row(it, k).wait_send()
        return carry

    lax.fori_loop(0, ITERS, drain, 0)


def body(right_side, diag_term, near_pairs, near_tiles, far_pairs, far_factors):
    k_near, k_far = near_tiles.shape[0], far_factors.shape[0]
    field = jax.ShapeDtypeStruct((4, 32, 256), F32)
    vmem = pl.BlockSpec(memory_space=pltpu.VMEM)
    hbm = pl.BlockSpec(memory_space=pl.ANY)
    xa, ra = pl.pallas_call(
        kernel,
        out_shape=(field, field),
        in_specs=[vmem, vmem, vmem, vmem, hbm, hbm],
        out_specs=(vmem, vmem),
        scratch_shapes=[
            pltpu.VMEM((k_near, 256, 256), BF16),
            pltpu.VMEM((k_near, 256, 256), BF16),
            pltpu.VMEM((k_far, 2, 32, 256), BF16),
            pltpu.VMEM((k_near + 1, 32, 256), F32),
            pltpu.VMEM((k_far + 1, 32, 256), F32),
            pltpu.VMEM((k_near + 1, 32, 256), F32),
            pltpu.VMEM((k_far + 1, 32, 256), F32),
            pltpu.VMEM((ITERS, 32, 32, 256), BF16),
            pltpu.VMEM((ITERS, 32, 32, 256), BF16),
            pltpu.VMEM((64, 32, 256), BF16),
            pltpu.VMEM((64, 32, 256), F32),
            pltpu.VMEM((ITERS, 2, 4, 4, 32, 256), BF16),
            pltpu.VMEM((ITERS, 2, 4, 4, 32, 256), BF16),
            pltpu.VMEM((ITERS, 4, 4, 32, 256), BF16),
            pltpu.VMEM((ITERS, 4, 4, 32, 256), BF16),
            pltpu.VMEM((ITERS, 3, 4, 32, 256), BF16),
            pltpu.VMEM((ITERS, 3, 4, 32, 256), BF16),
            pltpu.VMEM((ITERS, 3, 4, 32, 256), BF16),
            pltpu.VMEM((ITERS, 4, 32, 256), BF16),
            pltpu.VMEM((ITERS, 4, 32, 256), BF16),
            pltpu.VMEM((ITERS, 4, 32, 256), BF16),
            pltpu.VMEM((ITERS, 3, 4, 32, 256), BF16),
            pltpu.VMEM((ITERS, 8, 1, 128), F32),
            pltpu.VMEM((ITERS, 16, 1, 128), F32),
            pltpu.VMEM((4, 32, 256), F32),
            pltpu.VMEM((4, 32, 256), F32),
            pltpu.VMEM((2, 32, 128), F32),
            pltpu.VMEM((2, 32, 128), F32),
            pltpu.VMEM((32, 256), F32),
            pltpu.VMEM((8, 128), jnp.int32),
            pltpu.VMEM((16, 128), jnp.int32),
            pltpu.SMEM((16, 128), jnp.int32),
            pltpu.SemaphoreType.DMA((ITERS, N_SEM)),
            pltpu.SemaphoreType.DMA((ITERS, N_SEM)),
            pltpu.SemaphoreType.DMA((3,)),
        ],
        compiler_params=pltpu.CompilerParams(
            collective_id=0, has_side_effects=True, vmem_limit_bytes=60 * 2**20
        ),
    )(right_side, diag_term, near_pairs, far_pairs, near_tiles, far_factors)

    def tail(a, b, c, d):
        c[...] = a[...]
        d[...] = b[...]

    return pl.pallas_call(tail, out_shape=(field, field), in_specs=[vmem, vmem], out_specs=(vmem, vmem))(xa, ra)


def solution(mesh):
    placed = (
        P(("row", "col"), None, None),
        P(("row", "col"), None),
        P(None, ("row", "col")),
        P(("row", "col"), None, None),
        P(None, ("row", "col")),
        P(("row", "col"), None, None, None),
    )
    return jax.shard_map(
        body,
        mesh=mesh,
        in_specs=placed,
        out_specs=(P(("row", "col"), None, None), P(("row", "col"), None, None)),
        check_vma=False,
    )
```
